32 devices in a mesh: tile: 16 (over z, y, x), nrn: 2 (over core).
Axes of the slice: x: 2, y: 2, z: 4, core: 2. Of those that a mesh axis runs over, the one named last changes fastest.
Arguments:
- movie: bfloat16 [2, 128, 1024, 1024], P('nrn', 'tile'), may hold values from 0.099609375 to 2
- shifts: int32 [2, 128, 2], P('nrn', 'tile'), may hold values from -4 to 4
- footprints: bfloat16 [1536, 16, 128], P('tile'), may hold values from 0.019897461 to 1
- blocks: int32 [1536, 16], P('tile'), may hold values from 0 to 18431, as said below
- traces: float32 [2, 1536, 4], P('nrn', 'tile'), may hold values from 0.1 to 2
- counts: int32 [16], P('tile'), may hold values from 24 to 96, as said below
Outputs:
- new_traces: float32 [2, 1536, 4], P('nrn', 'tile')
- new_footprints: bfloat16 [1536, 16, 128], P('tile')
The draws below stay inside these ranges and needn't reach their ends.
Inputs may be any that keep to these rules, and one draw needn't show every extreme that they name: Each neuron has a plane z < 29, a block row r < 8 and a block column x < 63; blocks[k, 4 a + 2 d + e] = ((z + a) * 9 + r + d) * 64 + x + e for a in 0..3 and d, e in 0..1, so a neuron covers 2 x 2 blocks on each of 4 planes and reaches at most one block row below its tile's rows. `counts`: some tile is full and some holds 24 live neurons in every draw.
All inputs are finite; a program needn't handle non-finite values.
Results may differ from the reference program's by a relative error of at most 0.00105.
Values may be sent and summed in bfloat16 or wider, within the bound.
A program may use at most 256 MiB of HBM per device.

```python
import math
import jax
import jax.numpy as jnp
from jax import lax

H = 1024
W = 1024
Z = 32
NB = 16
PR = 8
PC = 16
VOX = 128
KT = 96
FH = 4
ZF = 128
PB = 8
RB = 9
XB = 64
TILES = 16
NEURONS = 1536


def draw_blocks(key, part):
    base = jax.random.fold_in(key, 11)
    key_plane, key_row, key_col = jax.random.split(base, 3)
    plane = jax.random.randint(key_plane, (NEURONS,), 0, Z - 3)
    row_start = jax.random.randint(key_row, (NEURONS,), 0, PB)
    column = jax.random.randint(key_col, (NEURONS,), 0, XB - 1)
    plane = plane.at[0].set(Z - 4).at[1].set(0)
    row_start = row_start.at[0].set(PB - 1).at[1].set(0)
    column = column.at[0].set(XB - 2).at[1].set(0)
    slot_index = jnp.arange(NB, dtype=jnp.int32)
    plane_step = slot_index // 4
    row_step = slot_index // 2 % 2
    col_step = slot_index % 2
    planes_all = plane[:, None] + plane_step[None, :]
    rows_all = row_start[:, None] + row_step[None, :]
    cols_all = column[:, None] + col_step[None, :]
    return ((planes_all * RB + rows_all) * XB + cols_all).astype(jnp.int32)


def draw_counts(key, part):
    base = jax.random.fold_in(key, 23)
    key_count, key_order = jax.random.split(base, 2)
    values = jax.random.randint(key_count, (TILES,), KT // 4, KT + 1)
    order = jax.random.permutation(key_order, TILES)
    values = values.at[order[0]].set(KT).at[order[1]].set(KT // 4)
    return values.astype(jnp.int32)


def plant(entries, own_key, low, high):
    longest = entries.shape.index(max(entries.shape))
    spots = []
    for shift in (0, 1):
        where = [jax.random.randint(jax.random.fold_in(own_key, axis), (), 0, length) for axis, length in enumerate(entries.shape)]
        where[longest] = (where[longest] + shift) % entries.shape[longest]
        spots.append(tuple(where))
    return entries.at[spots[0]].set(low).at[spots[1]].set(high)


def steps_of(key, shape, shards, smallest, high):
    def one(position, blocks):
        steps = jax.random.uniform(jax.random.fold_in(jax.random.fold_in(key, 6), position), (blocks,), jnp.float32, smallest / len(shards), high / len(shards))
        return jnp.repeat(jnp.exp(steps), shape[position] // blocks).reshape((-1,) + (1,) * (len(shape) - position - 1))

    factor_of = one(*shards[0])
    for cut in shards[1:]:
        factor_of = factor_of * one(*cut)
    return factor_of


def setup_inputs(seed: int = 0) -> dict:
    key_of = jax.random.split(jax.random.key(seed), 7)
    return {
        "movie": jnp.clip(0.099609375 + 1.9003906 * jax.random.uniform(key_of[0], (2, ZF, H, W), jnp.float32) ** steps_of(key_of[0], (2, ZF, H, W), ((0, 2), (1, 16)), -0.2, 0.2), 0.099609375, 2.0).astype(jnp.bfloat16),
        "shifts": plant(jax.random.randint(key_of[1], (2, ZF, 2), -4, 5), jax.random.fold_in(key_of[1], 1), -4, 4).astype(jnp.int32),
        "footprints": jnp.clip(jnp.exp(math.log(1.0) - 3.9171631 * jax.random.uniform(key_of[2], (NEURONS, NB, VOX), jnp.float32) ** steps_of(key_of[2], (NEURONS, NB, VOX), ((0, 16),), -0.2, 0.2)), 0.019897461, 1.0).astype(jnp.bfloat16),
        "blocks": draw_blocks(jax.random.fold_in(key_of[6], 71), 0),
        "traces": jnp.clip(jnp.exp(math.log(2.0) - 2.9957323 * jax.random.uniform(key_of[4], (2, NEURONS, FH), jnp.float32) ** steps_of(key_of[4], (2, NEURONS, FH), ((0, 2), (1, 16)), -0.2, 0.2)), 0.1, 2.0),
        "counts": draw_counts(jax.random.fold_in(key_of[6], 71), 0),
    }


EPSILON = 1e-6


def register(movie, shifts):
    row_index = jnp.arange(H, dtype=jnp.int32)
    col_index = jnp.arange(W, dtype=jnp.int32)

    def single(picture, offset):
        shifted = jnp.roll(picture, offset[0], axis=0)
        shifted = jnp.roll(shifted, offset[1], axis=1)
        inside_rows = (row_index - offset[0] >= 0) & (row_index - offset[0] < H)
        inside_cols = (col_index - offset[1] >= 0) & (col_index - offset[1] < W)
        inside = inside_rows[:, None] & inside_cols[None, :]
        return jnp.where(inside, shifted, jnp.zeros_like(shifted))

    return jax.vmap(jax.vmap(single))(movie, shifts)


def global_ids(blocks, tile_of):
    plane = blocks // (RB * XB)
    row_in = (blocks // XB) % RB
    column = blocks % XB
    return ((plane * (H // PR + 1) + tile_of[:, None] * PB + row_in) * XB + column).astype(jnp.int32)


def rebuild(masked, trace_all, global_id):
    accumulated = jnp.zeros((Z * (H // PR + 1) * XB, 2, FH, VOX), jnp.float32)

    def scan_step(accumulated, tile_item):
        footprint_tile, trace_tile, tile_ids = tile_item
        contrib = footprint_tile[:, :, None, None, :] * trace_tile[:, None, :, :, None]
        accumulated = accumulated.at[tile_ids.reshape(-1)].add(contrib.reshape(-1, 2, FH, VOX))
        return accumulated, None

    accumulated, _ = lax.scan(scan_step, accumulated,
                              (masked.reshape(TILES, KT, NB, VOX),
                               trace_all.reshape(TILES, KT, 2, FH),
                               global_id.reshape(TILES, KT, NB)))
    return accumulated


def project(recon_field, masked, global_id):
    def single(tile_item):
        footprint_tile, tile_ids = tile_item
        picked = recon_field[tile_ids].astype(jnp.float32)
        return jnp.einsum('kbv,kbpjv->kpj', footprint_tile, picked, precision=lax.Precision.HIGHEST)

    result = lax.map(single, (masked.reshape(TILES, KT, NB, VOX), global_id.reshape(TILES, KT, NB)))
    return result.reshape(NEURONS, 2, FH)


def spread(recon_field, trace_all, global_id):
    def single(tile_item):
        trace_tile, tile_ids = tile_item
        picked = recon_field[tile_ids].astype(jnp.float32)
        return jnp.einsum('kbpjv,kpj->kbv', picked, trace_tile, precision=lax.Precision.HIGHEST)

    result = lax.map(single, (trace_all.reshape(TILES, KT, 2, FH), global_id.reshape(TILES, KT, NB)))
    return result.reshape(NEURONS, NB, VOX)


def reference(movie, shifts, footprints, blocks, traces, counts):
    registered = register(movie, shifts)
    stacked = registered.reshape(2, Z, FH, H, W)
    stacked = jnp.pad(stacked, ((0, 0), (0, 0), (0, 0), (0, PR), (0, 0)))
    stacked = stacked.reshape(2, Z, FH, H // PR + 1, PR, XB, PC)
    field_movie = jnp.transpose(stacked, (1, 3, 5, 0, 2, 4, 6)).reshape(Z * (H // PR + 1) * XB, 2, FH, VOX)
    slot_index = jnp.arange(NEURONS, dtype=jnp.int32)
    tile_of = (slot_index // KT).astype(jnp.int32)
    alive = (slot_index % KT) < counts[tile_of]
    masked = jnp.where(alive[:, None, None], footprints, jnp.zeros_like(footprints)).astype(jnp.float32)
    global_id = global_ids(blocks, tile_of)
    old_traces = jnp.transpose(traces, (1, 0, 2))
    rebuilt = rebuild(masked, old_traces, global_id)
    numer_c = project(field_movie, masked, global_id)
    denom_c = project(rebuilt, masked, global_id) + EPSILON
    updated = old_traces * numer_c / denom_c
    rebuilt_new = rebuild(masked, updated, global_id)
    numer_a = spread(field_movie, updated, global_id)
    denom_a = spread(rebuilt_new, updated, global_id) + EPSILON
    new_footprints = (masked * numer_a / denom_a).astype(jnp.bfloat16)
    new_traces = jnp.transpose(updated, (1, 0, 2))
    return new_traces, new_footprints
```

```python
import functools

import jax
import jax.numpy as jnp
from jax import lax
from jax.experimental import pallas as pl
from jax.experimental.pallas import tpu as pltpu
from jax.sharding import PartitionSpec as P

Z = 32
PR = 8
PC = 16
VOX = 128
NB = 16
SPAN = 4
LANES = 128
WIN_R = 2 * PR
WIN_C = 2 * PC
EPSILON = 1e-06
MIB = 1 << 20
EXACT = lax.Precision.HIGHEST


def extract_kernel(
    cap, tiles, frames, height, width,
    rows_ref, cols_ref, bounds_ref, shift_ref, group_ref, movie_ref, out_ref, scr,
):
    d = pl.program_id(0)
    planes = pl.num_programs(0)

    @pl.when(d == 0)
    def _():
        out_ref[...] = jnp.zeros_like(out_ref)
        for f in range(frames):
            scr[f, pl.ds(0, 8), :] = jnp.zeros((8, width + 256), jnp.float32)
            scr[f, pl.ds(height + 8, 16), :] = jnp.zeros((16, width + 256), jnp.float32)

            @pl.loop(0, height // 64)
            def _(i):
                at = pl.ds(pl.multiple_of(i * 64 + 8, 8), 64)
                scr[f, at, pl.ds(0, 128)] = jnp.zeros((64, 128), jnp.float32)
                scr[f, at, pl.ds(width + 128, 128)] = jnp.zeros((64, 128), jnp.float32)

    for f in range(frames):

        @pl.loop(0, height // 32)
        def _(i):
            part = movie_ref[f, pl.ds(pl.multiple_of(i * 32, 32), 32), :]
            scr[f, pl.ds(pl.multiple_of(i * 32 + 8, 8), 32), pl.ds(128, width)] = part.astype(jnp.float32)

    lane = lax.broadcasted_iota(jnp.int32, (WIN_R, LANES), 1)
    row = lax.broadcasted_iota(jnp.int32, (WIN_R, LANES), 0)
    tall_lane = lax.broadcasted_iota(jnp.int32, (WIN_R + 8, LANES), 1)
    first = group_ref[0] * frames
    moves = [(shift_ref[2 * (d * frames + f)], shift_ref[2 * (d * frames + f) + 1]) for f in range(frames)]

    @pl.loop(0, tiles)
    def _(t):
        low = bounds_ref[t * (planes + 1) + d]
        high = bounds_ref[t * (planes + 1) + d + 1]

        def one(c, carry):
            slot = t * cap + c
            r0 = rows_ref[slot]
            c0 = cols_ref[slot]
            window = jnp.zeros((WIN_R, LANES), jnp.float32)
            for f in range(frames):
                down, right = moves[f]
                top = r0 - down + 8
                left = c0 - right + 128
                m = lax.shift_right_logical(left, 7)
                o = left - m * 128
                k = top & 7
                at = pl.ds(pl.multiple_of(top - k, 8), WIN_R + 8)
                near = scr[f, at, pl.ds(pl.multiple_of(m * 128, 128), 128)]
                far = scr[f, at, pl.ds(pl.multiple_of(m * 128 + 128, 128), 128)]
                place = (first + f) * WIN_C
                both = jnp.where(tall_lane >= o, near, far)
                parts = []
                for i in range(0, WIN_R, 8):
                    part = jnp.where(row[:8] >= k, both[i : i + 8], both[i + 8 : i + 16])
                    part = pltpu.roll(part, (8 - k) & 7, 0)
                    parts.append(pltpu.roll(part, (place - o + 128) & 127, 1))
                both = jnp.concatenate(parts, axis=0)
                window = jnp.where((lane >= place) & (lane < place + WIN_C), both, window)
            window = jnp.where(row + r0 < height, window, 0.0)
            out_ref[slot] = window.astype(jnp.bfloat16)
            return carry

        lax.fori_loop(low, high, one, 0)


def extract(movie, shifts, rows, cols, bounds, group, cap, tiles, frames):
    images, height, width = movie.shape
    planes = images // frames
    smem = pl.BlockSpec(memory_space=pltpu.SMEM)
    return pl.pallas_call(
        functools.partial(extract_kernel, cap, tiles, frames, height, width),
        grid=(planes,),
        in_specs=[smem] * 5 + [pl.BlockSpec((frames, height, width), lambda d: (d, 0, 0))],
        out_specs=pl.BlockSpec((tiles * cap, WIN_R, LANES), lambda d: (0, 0, 0)),
        out_shape=jax.ShapeDtypeStruct((tiles * cap, WIN_R, LANES), jnp.bfloat16),
        scratch_shapes=[pltpu.VMEM((frames, height + 24, width + 256), jnp.float32)],
        compiler_params=pltpu.CompilerParams(vmem_limit_bytes=56 * MIB),
        name="extract_windows",
    )(rows.reshape(-1), cols.reshape(-1), bounds.reshape(-1), shifts.reshape(-1), group.reshape(1), movie)


def overlap_kernel(own_ref, own_ids_ref, cols_ref, col_ids_ref, traces_ref, out_ref, acc):
    b = pl.program_id(0)
    products = lax.dot_general(
        own_ref[...], cols_ref[...], (((1,), (1,)), ((), ())), preferred_element_type=jnp.float32
    )
    kept = jnp.where(own_ids_ref[0] == col_ids_ref[...], products, 0.0)

    @pl.when(b == 0)
    def _():
        acc[...] = kept

    @pl.when(b > 0)
    def _():
        acc[...] += kept

    @pl.when(b == pl.num_programs(0) - 1)
    def _():
        out_ref[...] = (
            jnp.dot(acc[...], traces_ref[...], precision=EXACT, preferred_element_type=jnp.float32) + EPSILON
        )


def whole_spec(shape):
    return pl.BlockSpec(shape, lambda i: (0,) * len(shape))


def overlaps(own, own_ids, cols, col_ids, col_traces):
    slots = own.shape[0]
    width = cols.shape[0]
    return pl.pallas_call(
        overlap_kernel,
        grid=(NB,),
        in_specs=[
            pl.BlockSpec((slots, VOX), lambda b: (0, b)),
            pl.BlockSpec((1, slots, 1), lambda b: (b, 0, 0)),
            whole_spec(cols.shape),
            whole_spec(col_ids.shape),
            whole_spec(col_traces.shape),
        ],
        out_specs=whole_spec((slots, LANES)),
        out_shape=jax.ShapeDtypeStruct((slots, LANES), jnp.float32),
        scratch_shapes=[pltpu.VMEM((slots, width), jnp.float32)],
        compiler_params=pltpu.CompilerParams(vmem_limit_bytes=32 * MIB),
        name="denom_c",
    )(own, own_ids, cols, col_ids, col_traces)


def update_kernel(picked_ref, masked_ref, traces_ref, denom_ref, new_ref, numer_ref):
    pairs = masked_ref.shape[0]
    slots = traces_ref.shape[0]
    keep_lane = lax.broadcasted_iota(jnp.int32, (pairs, PR, 2 * VOX), 2)
    keep_row = lax.broadcasted_iota(jnp.int32, (pairs, PR, 2 * VOX), 1)
    keep = (keep_lane & (VOX - 1)) // PC == keep_row
    out_lane = lax.broadcasted_iota(jnp.int32, (LANES, 2 * VOX), 1)
    in_lane = lax.broadcasted_iota(jnp.int32, (LANES, 2 * VOX), 0)
    fold = ((in_lane & (WIN_C - 1)) == (out_lane // VOX) * PC + (out_lane & (PC - 1))).astype(jnp.bfloat16)
    group_a = lax.broadcasted_iota(jnp.int32, (LANES, LANES), 0) // WIN_C
    group_b = lax.broadcasted_iota(jnp.int32, (LANES, LANES), 1) // WIN_C
    group_sum = (group_a == group_b).astype(jnp.float32)

    feet = masked_ref[...].astype(jnp.float32)
    feet = jnp.where(keep, feet[:, None, :], 0.0).reshape(pairs * PR, 2 * VOX).astype(jnp.bfloat16)
    feet = lax.dot_general(feet, fold, (((1,), (1,)), ((), ())), preferred_element_type=jnp.float32)
    seen = picked_ref[...].astype(jnp.float32)
    sums = (feet * seen).reshape(slots, SPAN * WIN_R, LANES).sum(axis=1)
    numer_c = jnp.dot(sums, group_sum, precision=EXACT, preferred_element_type=jnp.float32)
    new = traces_ref[...] * numer_c / denom_ref[...]
    new_ref[...] = new
    scaled = (seen.reshape(slots, SPAN * WIN_R, LANES) * new[:, None, :]).reshape(pairs * PR, LANES)
    high = scaled.astype(jnp.bfloat16)
    low = (scaled - high.astype(jnp.float32)).astype(jnp.bfloat16)
    spread = jnp.dot(high, fold, preferred_element_type=jnp.float32)
    spread += jnp.dot(low, fold, preferred_element_type=jnp.float32)
    numer_ref[...] = jnp.where(keep, spread.reshape(pairs, PR, 2 * VOX), 0.0).sum(axis=1)


def update(picked, masked, traces, denom):
    slots = traces.shape[0]
    step = 8
    pairs = step * SPAN * 2
    trace_spec = pl.BlockSpec((step, LANES), lambda i: (i, 0))
    pair_spec = pl.BlockSpec((pairs, 2 * VOX), lambda i: (i, 0))
    return pl.pallas_call(
        update_kernel,
        grid=(slots // step,),
        in_specs=[pl.BlockSpec((pairs * PR, LANES), lambda i: (i, 0)), pair_spec, trace_spec, trace_spec],
        out_specs=[trace_spec, pair_spec],
        out_shape=[
            jax.ShapeDtypeStruct((slots, LANES), jnp.float32),
            jax.ShapeDtypeStruct((slots * SPAN * 2, 2 * VOX), jnp.float32),
        ],
        compiler_params=pltpu.CompilerParams(vmem_limit_bytes=32 * MIB),
        name="update_traces",
    )(picked, masked, traces, denom)


def finish_kernel(
    own_ref, own_ids_ref, cols_ref, col_ids_ref, traces_ref, col_traces_ref, mine_ref, other_ref, out_ref, pair
):
    @pl.when(pl.program_id(0) == 0)
    def _():
        pair[...] = lax.dot_general(
            traces_ref[...], col_traces_ref[...], (((1,), (1,)), ((), ())),
            precision=EXACT, preferred_element_type=jnp.float32,
        )

    weight = jnp.where(own_ids_ref[0] == col_ids_ref[...], pair[...], 0.0)
    high = weight.astype(jnp.bfloat16)
    low = (weight - high.astype(jnp.float32)).astype(jnp.bfloat16)
    denom = jnp.dot(high, cols_ref[...], preferred_element_type=jnp.float32)
    denom += jnp.dot(low, cols_ref[...], preferred_element_type=jnp.float32)
    numer = mine_ref[...] + other_ref[...]
    out_ref[...] = (own_ref[...].astype(jnp.float32) * numer / (denom + EPSILON)).astype(jnp.bfloat16)


def finish(own, own_ids, cols, col_ids, traces, col_traces, mine, other):
    slots = own.shape[0]
    width = cols.shape[0]
    block = pl.BlockSpec((slots, VOX), lambda b: (0, b))
    return pl.pallas_call(
        finish_kernel,
        grid=(NB,),
        in_specs=[
            block,
            pl.BlockSpec((1, slots, 1), lambda b: (b, 0, 0)),
            whole_spec(cols.shape),
            whole_spec(col_ids.shape),
            whole_spec(traces.shape),
            whole_spec(col_traces.shape),
            block,
            block,
        ],
        out_specs=block,
        out_shape=jax.ShapeDtypeStruct((slots, NB * VOX), jnp.bfloat16),
        scratch_shapes=[pltpu.VMEM((slots, width), jnp.float32)],
        compiler_params=pltpu.CompilerParams(vmem_limit_bytes=32 * MIB),
        name="new_footprints",
    )(own, own_ids, cols, col_ids, traces, col_traces, mine, other)


def shards(movie, shifts, footprints, blocks, traces, counts):
    images, height, width = movie.shape[1:]
    tiles, me = lax.axis_size("tile"), lax.axis_index("tile")
    band = height // tiles
    pb = band // PR
    rb, xb = pb + 1, width // PC
    fh, slots = traces.shape[2], footprints.shape[0]
    frames = min(images, fh)
    planes = images // frames
    groups = fh // frames
    cap = 24 * planes
    ups = [(i, i + 1) for i in range(tiles - 1)]
    downs = [(i + 1, i) for i in range(tiles - 1)]

    info = lax.all_gather(jnp.concatenate([blocks[:, 0], counts]), "tile")
    base, live_count = info[:, :slots], info[:, slots:]
    z, r, x = base // (rb * xb), (base // xb) % rb, base % xb
    live = jnp.arange(slots, dtype=jnp.int32) < live_count
    plane_ids = jnp.arange(Z, dtype=jnp.int32)
    cover = live[:, None, :] & (z[:, None, :] <= plane_ids[:, None]) & (plane_ids[:, None] < z[:, None, :] + SPAN)
    before = jnp.triu(jnp.ones((slots, slots), jnp.bfloat16), 1)
    rank = jnp.einsum(
        "tzk,kj->tzj", cover.astype(jnp.bfloat16), before, preferred_element_type=jnp.float32
    ).astype(jnp.int32)
    totals = cover.sum(axis=2, dtype=jnp.int32).reshape(tiles, Z // planes, planes)
    ends = jnp.cumsum(totals, axis=2) if planes > 1 else totals
    starts = (ends - totals).reshape(tiles, Z)
    place = rank + starts[:, :, None]
    rounds = (jnp.max(ends) + cap - 1) // cap

    first_plane = (me // groups) * planes
    my_cover = lax.dynamic_slice_in_dim(cover, first_plane, planes, 1)
    my_place = jnp.where(my_cover, lax.dynamic_slice_in_dim(place, first_plane, planes, 1), -1)
    my_ends = lax.dynamic_slice_in_dim(ends, me // groups, 1, 1)[:, 0]
    bounds = jnp.concatenate([jnp.zeros((tiles, 1), jnp.int32), my_ends], axis=1)
    row_start = jnp.arange(tiles, dtype=jnp.int32)[:, None] * band + PR * r
    col_start = PC * x
    own_z = blocks[:, 0] // (rb * xb)
    own_live = jnp.arange(slots, dtype=jnp.int32) < counts[0]
    own_plane = own_z[:, None] + jnp.arange(SPAN, dtype=jnp.int32)
    own_place = lax.dynamic_index_in_dim(place, me, 0, False)
    own_place = jnp.where(own_plane[:, :, None] == plane_ids, own_place.T[:, None, :], 0).sum(axis=2)
    source = (own_plane // planes) * groups

    def one_round(number, picked):
        offset = number * cap
        slot_ids = jnp.arange(cap, dtype=jnp.int32) + offset
        hit = my_place[:, None] == slot_ids[:, None, None]
        rows = jnp.where(hit, row_start[:, None, None, :], 0).sum(axis=(2, 3))
        cols = jnp.where(hit, col_start[:, None, None, :], 0).sum(axis=(2, 3))
        limits = jnp.clip(bounds - offset, 0, cap)
        sent = extract(movie[0], shifts[0], rows, cols, limits, me % groups, cap, tiles, frames)
        received = lax.all_to_all(sent, "tile", split_axis=0, concat_axis=0, tiled=True)
        local = own_place - offset
        valid = own_live[:, None] & (local >= 0) & (local < cap)
        safe = jnp.clip(local, 0, cap - 1)
        fresh = 0
        for g in range(groups):
            fresh = fresh + jnp.take(received, (source + g) * cap + safe, axis=0)
        old = jnp.zeros_like(fresh) if picked is None else picked
        return jnp.where(valid[:, :, None, None], fresh, old)

    masked = jnp.where(own_live[:, None, None], footprints, jnp.zeros_like(footprints))
    halves = masked.reshape(slots, SPAN, 2, 2, VOX)
    by_block = lambda part: jnp.transpose(part, (1, 2, 0, 3)).reshape(-1, VOX)
    top = by_block(halves[:, :, 0])
    bottom = by_block(halves[:, :, 1])
    above = lax.ppermute(bottom, "tile", ups)
    below = lax.ppermute(top, "tile", downs)
    own_traces = traces[0]
    trace_above = lax.ppermute(own_traces, "tile", ups)
    trace_below = lax.ppermute(own_traces, "tile", downs)
    cols = jnp.concatenate([jnp.transpose(masked, (1, 0, 2)).reshape(-1, VOX), above, below], axis=0)

    def edge_ids(neighbour, d, row, shift):
        base_there = lax.dynamic_index_in_dim(base, jnp.clip(neighbour, 0, tiles - 1), 0, False)
        row_there = (base_there // xb) % rb + d
        steps = (jnp.arange(SPAN)[:, None] * rb * xb + d * xb + jnp.arange(2)).reshape(-1, 1).astype(jnp.int32)
        good = (row_there == row) & (neighbour >= 0) & (neighbour < tiles)
        return jnp.where(good, base_there + steps + shift, -1).reshape(-1)

    col_ids = jnp.concatenate(
        [blocks.T.reshape(-1), edge_ids(me - 1, 1, pb, -pb * xb), edge_ids(me + 1, 0, 0, pb * xb)]
    )[None]
    own_ids = blocks.T[:, :, None]
    own_flat = masked.reshape(slots, NB * VOX)

    def columns(own, up, down):
        return jnp.concatenate([jnp.tile(own, (NB, 1)), jnp.tile(up, (NB // 2, 1)), jnp.tile(down, (NB // 2, 1))])

    wide = lambda part: jnp.repeat(part, LANES // fh, axis=1)
    denom_c = overlaps(
        own_flat, own_ids, cols, col_ids, columns(wide(own_traces), wide(trace_above), wide(trace_below))
    )

    picked = one_round(0, None)
    _, picked = lax.while_loop(
        lambda state: state[0] < rounds,
        lambda state: (state[0] + 1, one_round(state[0], state[1])),
        (jnp.int32(1), picked),
    )
    new_wide, numer = update(
        picked.reshape(-1, LANES), masked.reshape(slots * SPAN * 2, 2 * VOX), wide(own_traces), denom_c
    )
    new = new_wide[:, :: LANES // fh]

    def across(part, step):
        pairs = [
            (t * 2 + p, (t + step) * 2 + 1 - p) for t in range(tiles) for p in range(2) if 0 <= t + step < tiles
        ]
        return lax.ppermute(part, ("tile", "nrn"), pairs)

    numer_other = across(numer, 0)
    low_parity = lax.axis_index("nrn") == 0

    def all_frames(mine, other):
        both = jnp.where(low_parity, jnp.concatenate([mine, other], 1), jnp.concatenate([other, mine], 1))
        return jnp.pad(both, ((0, 0), (0, LANES - 2 * fh)))

    new_all = all_frames(new, across(new, 0))
    new_above = all_frames(lax.ppermute(new, "tile", ups), across(new, 1))
    new_below = all_frames(lax.ppermute(new, "tile", downs), across(new, -1))
    new_footprints = finish(
        own_flat, own_ids, cols, col_ids, new_all, columns(new_all, new_above, new_below),
        numer.reshape(slots, NB * VOX), numer_other.reshape(slots, NB * VOX),
    )
    return (new[None], new_footprints.reshape(slots, NB, VOX))


def solution(mesh):
    placed = (
        P("nrn", "tile", None, None),
        P("nrn", "tile", None),
        P("tile", None, None),
        P("tile", None),
        P("nrn", "tile", None),
        P("tile"),
    )
    return jax.shard_map(
        shards,
        mesh=mesh,
        in_specs=placed,
        out_specs=(P("nrn", "tile", None), P("tile", None, None)),
        check_vma=False,
    )
```

```python
import functools

import jax
import jax.numpy as jnp
from jax import lax
from jax.experimental import pallas as pl
from jax.experimental.pallas import tpu as pltpu
from jax.sharding import PartitionSpec as P

Z = 32
PR = 8
PC = 16
VOX = 128
NB = 16
SPAN = 4
LANES = 128
WIN_R = 2 * PR
WIN_C = 2 * PC
EPSILON = 1e-06
MIB = 1 << 20
EXACT = lax.Precision.HIGHEST


def extract_kernel(
    cap, step, tiles, plane, frames, height, width,
    rows_ref, cols_ref, counts_ref, shift_ref, group_ref, movie_ref, out_ref, scr,
):
    frame = pl.program_id(0)

    scr[frame, pl.ds(0, 8), :] = jnp.zeros((8, width + 256), jnp.float32)
    scr[frame, pl.ds(height + 8, 16), :] = jnp.zeros((16, width + 256), jnp.float32)

    @pl.loop(0, height // 32)
    def _(i):
        at = pl.ds(pl.multiple_of(i * 32 + 8, 8), 32)
        scr[frame, at, pl.ds(0, 128)] = jnp.zeros((32, 128), jnp.float32)
        scr[frame, at, pl.ds(width + 128, 128)] = jnp.zeros((32, 128), jnp.float32)
        part = movie_ref[0, pl.ds(pl.multiple_of(i * 32, 32), 32), :]
        scr[frame, at, pl.ds(128, width)] = part.astype(jnp.float32)

    @pl.when(frame == frames - 1)
    def _():
        out_ref[...] = jnp.zeros_like(out_ref)
        lane = lax.broadcasted_iota(jnp.int32, (WIN_R + 8, LANES), 1)
        row = lax.broadcasted_iota(jnp.int32, (WIN_R, LANES), 0)
        first = group_ref[0] * frames
        moves = [
            (shift_ref[2 * (plane * frames + f)], shift_ref[2 * (plane * frames + f) + 1]) for f in range(frames)
        ]

        def one(slot):
            r0 = rows_ref[slot]
            c0 = cols_ref[slot]
            window = jnp.zeros((WIN_R, LANES), jnp.float32)
            for f in range(frames):
                down, right = moves[f]
                top = r0 - down + 8
                left = c0 - right + 128
                m = lax.shift_right_logical(left, 7)
                o = left - m * 128
                k = top & 7
                at = pl.ds(pl.multiple_of(top - k, 8), WIN_R + 8)
                near = scr[f, at, pl.ds(pl.multiple_of(m * 128, 128), 128)]
                far = scr[f, at, pl.ds(pl.multiple_of(m * 128 + 128, 128), 128)]
                place = (first + f) * WIN_C
                both = jnp.where(lane >= o, near, far)
                parts = []
                for i in range(0, WIN_R, 8):
                    part = jnp.where(row[:8] >= k, both[i : i + 8], both[i + 8 : i + 16])
                    part = pltpu.roll(part, (8 - k) & 7, 0)
                    parts.append(pltpu.roll(part, (place - o + 128) & 127, 1))
                both = jnp.concatenate(parts, axis=0)
                window = jnp.where((lane[:WIN_R] >= place) & (lane[:WIN_R] < place + WIN_C), both, window)
            return jnp.where(row + r0 < height, window, 0.0).astype(jnp.bfloat16)

        @pl.loop(0, tiles)
        def _(t):
            def some(i, carry):
                slots = [t * cap + i * step + j for j in range(step)]
                windows = [one(slot) for slot in slots]
                for slot, window in zip(slots, windows):
                    out_ref[slot] = window
                return carry

            lax.fori_loop(0, (counts_ref[t] + step - 1) // step, some, 0)


def extract(movie, shifts, rows, cols, counts, group, cap, step, tiles, plane, frames):
    _, height, width = movie.shape
    smem = pl.BlockSpec(memory_space=pltpu.SMEM)
    return pl.pallas_call(
        functools.partial(extract_kernel, cap, step, tiles, plane, frames, height, width),
        grid=(frames,),
        in_specs=[smem] * 5 + [pl.BlockSpec((1, height, width), lambda f: (plane * frames + f, 0, 0))],
        out_specs=pl.BlockSpec((tiles * cap, WIN_R, LANES), lambda f: (0, 0, 0)),
        out_shape=jax.ShapeDtypeStruct((tiles * cap, WIN_R, LANES), jnp.bfloat16),
        scratch_shapes=[pltpu.VMEM((frames, height + 24, width + 256), jnp.float32)],
        compiler_params=pltpu.CompilerParams(vmem_limit_bytes=56 * MIB),
        name="extract_windows",
    )(rows.reshape(-1), cols.reshape(-1), counts, shifts.reshape(-1), group.reshape(1), movie)


def exchange_kernel(tiles, new_ref, numer_ref, near_ref, other_ref, send_sem, recv_sem):
    t, p = lax.axis_index("tile"), lax.axis_index("nrn")
    q = 1 - p
    has_above, has_below = t > 0, t < tiles - 1
    mesh_id = pl.DeviceIdType.MESH
    barrier = pltpu.get_barrier_semaphore()
    pl.semaphore_signal(barrier, inc=1, device_id=(t, q), device_id_type=mesh_id)

    @pl.when(has_above)
    def _():
        for peer in (p, q):
            pl.semaphore_signal(barrier, inc=1, device_id=(t - 1, peer), device_id_type=mesh_id)

    @pl.when(has_below)
    def _():
        for peer in (p, q):
            pl.semaphore_signal(barrier, inc=1, device_id=(t + 1, peer), device_id_type=mesh_id)

    pl.semaphore_wait(barrier, 1 + 2 * has_above.astype(jnp.int32) + 2 * has_below.astype(jnp.int32))

    def copy(src, dst, i, to):
        return pltpu.make_async_remote_copy(
            src_ref=src, dst_ref=dst, send_sem=send_sem.at[i], recv_sem=recv_sem.at[i],
            device_id=to, device_id_type=mesh_id,
        )

    partner = copy(new_ref, near_ref.at[0], 0, (t, q))
    large = copy(numer_ref, other_ref, 5, (t, q))
    to_below = [copy(new_ref, near_ref.at[1 + i], 1 + i, (t + 1, peer)) for i, peer in enumerate((p, q))]
    to_above = [copy(new_ref, near_ref.at[3 + i], 3 + i, (t - 1, peer)) for i, peer in enumerate((p, q))]

    @pl.when(has_below)
    def _():
        for one in to_below:
            one.start()

    @pl.when(has_above)
    def _():
        for one in to_above:
            one.start()

    partner.start()
    large.start()

    @pl.when(has_below)
    def _():
        for one in to_below:
            one.wait_send()
        for one in to_above:
            one.wait_recv()

    @pl.when(has_above)
    def _():
        for one in to_above:
            one.wait_send()
        for one in to_below:
            one.wait_recv()

    partner.wait()
    large.wait()


def exchange(new, numer, tiles):
    anywhere = pl.BlockSpec(memory_space=pl.ANY)
    return pl.pallas_call(
        functools.partial(exchange_kernel, tiles),
        in_specs=[anywhere, anywhere],
        out_specs=[anywhere, anywhere],
        out_shape=[
            jax.ShapeDtypeStruct((5,) + new.shape, jnp.float32),
            jax.ShapeDtypeStruct(numer.shape, jnp.float32),
        ],
        scratch_shapes=[pltpu.SemaphoreType.DMA((6,)), pltpu.SemaphoreType.DMA((6,))],
        compiler_params=pltpu.CompilerParams(collective_id=0, has_side_effects=True),
        name="exchange",
    )(new, numer)


def overlap_kernel(own_ref, own_ids_ref, cols_ref, col_ids_ref, traces_ref, out_ref, acc):
    b = pl.program_id(0)
    products = lax.dot_general(
        own_ref[...], cols_ref[...], (((1,), (1,)), ((), ())), preferred_element_type=jnp.float32
    )
    kept = jnp.where(own_ids_ref[0] == col_ids_ref[...], products, 0.0)

    @pl.when(b == 0)
    def _():
        acc[...] = kept

    @pl.when(b > 0)
    def _():
        acc[...] += kept

    @pl.when(b == pl.num_programs(0) - 1)
    def _():
        out_ref[...] = (
            jnp.dot(acc[...], traces_ref[...], precision=EXACT, preferred_element_type=jnp.float32) + EPSILON
        )


def whole_spec(shape):
    return pl.BlockSpec(shape, lambda i: (0,) * len(shape))


def overlaps(own, own_ids, cols, col_ids, col_traces):
    slots = own.shape[0]
    width = cols.shape[0]
    return pl.pallas_call(
        overlap_kernel,
        grid=(NB,),
        in_specs=[
            pl.BlockSpec((slots, VOX), lambda b: (0, b)),
            pl.BlockSpec((1, slots, 1), lambda b: (b, 0, 0)),
            whole_spec(cols.shape),
            whole_spec(col_ids.shape),
            whole_spec(col_traces.shape),
        ],
        out_specs=whole_spec((slots, LANES)),
        out_shape=jax.ShapeDtypeStruct((slots, LANES), jnp.float32),
        scratch_shapes=[pltpu.VMEM((slots, width), jnp.float32)],
        compiler_params=pltpu.CompilerParams(vmem_limit_bytes=32 * MIB),
        name="denom_c",
    )(own, own_ids, cols, col_ids, col_traces)


def update_kernel(picked_ref, masked_ref, traces_ref, denom_ref, new_ref, numer_ref):
    pairs = masked_ref.shape[0]
    slots = traces_ref.shape[0]
    keep_lane = lax.broadcasted_iota(jnp.int32, (pairs, PR, 2 * VOX), 2)
    keep_row = lax.broadcasted_iota(jnp.int32, (pairs, PR, 2 * VOX), 1)
    keep = (keep_lane & (VOX - 1)) // PC == keep_row
    out_lane = lax.broadcasted_iota(jnp.int32, (LANES, 2 * VOX), 1)
    in_lane = lax.broadcasted_iota(jnp.int32, (LANES, 2 * VOX), 0)
    fold = ((in_lane & (WIN_C - 1)) == (out_lane // VOX) * PC + (out_lane & (PC - 1))).astype(jnp.bfloat16)
    group_a = lax.broadcasted_iota(jnp.int32, (LANES, LANES), 0) // WIN_C
    group_b = lax.broadcasted_iota(jnp.int32, (LANES, LANES), 1) // WIN_C
    group_sum = (group_a == group_b).astype(jnp.float32)

    feet = masked_ref[...].astype(jnp.float32)
    feet = jnp.where(keep, feet[:, None, :], 0.0).reshape(pairs * PR, 2 * VOX).astype(jnp.bfloat16)
    feet = lax.dot_general(feet, fold, (((1,), (1,)), ((), ())), preferred_element_type=jnp.float32)
    seen = picked_ref[...].astype(jnp.float32)
    sums = (feet * seen).reshape(slots, SPAN * WIN_R, LANES).sum(axis=1)
    numer_c = jnp.dot(sums, group_sum, precision=EXACT, preferred_element_type=jnp.float32)
    new = traces_ref[...] * numer_c / denom_ref[...]
    new_ref[...] = new
    scaled = (seen.reshape(slots, SPAN * WIN_R, LANES) * new[:, None, :]).reshape(pairs * PR, LANES)
    high = scaled.astype(jnp.bfloat16)
    low = (scaled - high.astype(jnp.float32)).astype(jnp.bfloat16)
    spread = jnp.dot(high, fold, preferred_element_type=jnp.float32)
    spread += jnp.dot(low, fold, preferred_element_type=jnp.float32)
    numer_ref[...] = jnp.where(keep, spread.reshape(pairs, PR, 2 * VOX), 0.0).sum(axis=1)


def update(picked, masked, traces, denom):
    slots = traces.shape[0]
    step = 8
    pairs = step * SPAN * 2
    trace_spec = pl.BlockSpec((step, LANES), lambda i: (i, 0))
    pair_spec = pl.BlockSpec((pairs, 2 * VOX), lambda i: (i, 0))
    return pl.pallas_call(
        update_kernel,
        grid=(slots // step,),
        in_specs=[pl.BlockSpec((pairs * PR, LANES), lambda i: (i, 0)), pair_spec, trace_spec, trace_spec],
        out_specs=[trace_spec, pair_spec],
        out_shape=[
            jax.ShapeDtypeStruct((slots, LANES), jnp.float32),
            jax.ShapeDtypeStruct((slots * SPAN * 2, 2 * VOX), jnp.float32),
        ],
        compiler_params=pltpu.CompilerParams(vmem_limit_bytes=32 * MIB),
        name="update_traces",
    )(picked, masked, traces, denom)


def finish_kernel(
    own_ref, own_ids_ref, cols_ref, col_ids_ref, traces_ref, other_traces_ref, col_traces_ref, other_col_ref,
    mine_ref, other_ref, out_ref, pair,
):
    @pl.when(pl.program_id(0) == 0)
    def _():
        def products(left, right):
            return lax.dot_general(
                left[...], right[...], (((1,), (1,)), ((), ())), precision=EXACT, preferred_element_type=jnp.float32
            )

        both = products(traces_ref, col_traces_ref) + products(other_traces_ref, other_col_ref)
        pair[...] = both * (1.0 / WIN_C)

    weight = jnp.where(own_ids_ref[0] == col_ids_ref[...], pair[...], 0.0)
    high = weight.astype(jnp.bfloat16)
    low = (weight - high.astype(jnp.float32)).astype(jnp.bfloat16)
    denom = jnp.dot(high, cols_ref[...], preferred_element_type=jnp.float32)
    denom += jnp.dot(low, cols_ref[...], preferred_element_type=jnp.float32)
    numer = mine_ref[...] + other_ref[...]
    out_ref[...] = (own_ref[...].astype(jnp.float32) * numer / (denom + EPSILON)).astype(jnp.bfloat16)


def finish(own, own_ids, cols, col_ids, traces, other_traces, col_traces, other_col, mine, other):
    slots = own.shape[0]
    width = cols.shape[0]
    block = pl.BlockSpec((slots, VOX), lambda b: (0, b))
    return pl.pallas_call(
        finish_kernel,
        grid=(NB,),
        in_specs=[
            block,
            pl.BlockSpec((1, slots, 1), lambda b: (b, 0, 0)),
            whole_spec(cols.shape),
            whole_spec(col_ids.shape),
            whole_spec(traces.shape),
            whole_spec(traces.shape),
            whole_spec(col_traces.shape),
            whole_spec(col_traces.shape),
            block,
            block,
        ],
        out_specs=block,
        out_shape=jax.ShapeDtypeStruct((slots, NB * VOX), jnp.bfloat16),
        scratch_shapes=[pltpu.VMEM((slots, width), jnp.float32)],
        compiler_params=pltpu.CompilerParams(vmem_limit_bytes=32 * MIB),
        name="new_footprints",
    )(own, own_ids, cols, col_ids, traces, other_traces, col_traces, other_col, mine, other)


def shards(movie, shifts, footprints, blocks, traces, counts):
    images, height, width = movie.shape[1:]
    tiles, me = lax.axis_size("tile"), lax.axis_index("tile")
    band = height // tiles
    pb = band // PR
    rb, xb = pb + 1, width // PC
    fh, slots = traces.shape[2], footprints.shape[0]
    frames = min(images, fh)
    planes = images // frames
    groups = fh // frames
    cap, step = 25, 5
    ups = [(i, i + 1) for i in range(tiles - 1)]
    downs = [(i + 1, i) for i in range(tiles - 1)]

    info = lax.all_gather(jnp.concatenate([blocks[:, 0], counts]), "tile")
    base, live_count = info[:, :slots], info[:, slots:]
    z, r, x = base // (rb * xb), (base // xb) % rb, base % xb
    live = jnp.arange(slots, dtype=jnp.int32) < live_count
    plane_ids = jnp.arange(Z, dtype=jnp.int32)
    cover = live[:, None, :] & (z[:, None, :] <= plane_ids[:, None]) & (plane_ids[:, None] < z[:, None, :] + SPAN)
    before = jnp.triu(jnp.ones((slots, slots), jnp.bfloat16), 1)
    rank = jnp.einsum(
        "tzk,kj->tzj", cover.astype(jnp.bfloat16), before, preferred_element_type=jnp.float32
    ).astype(jnp.int32)
    totals = cover.sum(axis=2, dtype=jnp.int32)
    rounds = (jnp.max(totals) + cap - 1) // cap

    first_plane = (me // groups) * planes
    my_place = lax.dynamic_slice_in_dim(jnp.where(cover, rank, -1), first_plane, planes, 1)
    my_totals = lax.dynamic_slice_in_dim(totals, first_plane, planes, 1)
    row_start = jnp.arange(tiles, dtype=jnp.int32)[:, None] * band + PR * r
    col_start = PC * x
    own_z = blocks[:, 0] // (rb * xb)
    own_live = jnp.arange(slots, dtype=jnp.int32) < counts[0]
    own_plane = own_z[:, None] + jnp.arange(SPAN, dtype=jnp.int32)
    own_place = lax.dynamic_index_in_dim(rank, me, 0, False)
    own_place = jnp.where(own_plane[:, :, None] == plane_ids, own_place.T[:, None, :], 0).sum(axis=2)
    source = (own_plane // planes) * groups

    def one_round(number, picked):
        offset = number * cap
        slot_ids = jnp.arange(cap, dtype=jnp.int32) + offset
        hit = my_place[:, :, None] == slot_ids[:, None]
        rows = jnp.where(hit, row_start[:, None, None, :], 0).sum(axis=3)
        cols = jnp.where(hit, col_start[:, None, None, :], 0).sum(axis=3)
        limits = jnp.clip(my_totals - offset, 0, cap)
        local = own_place - offset
        valid = own_live[:, None] & (local >= 0) & (local < cap)
        safe = jnp.clip(local, 0, cap - 1)
        received = []
        for d in range(planes):
            sent = extract(
                movie[0], shifts[0], rows[:, d], cols[:, d], limits[:, d], me % groups, cap, step, tiles, d, frames
            )
            received.append(lax.all_to_all(sent, "tile", split_axis=0, concat_axis=0, tiled=True))
        for d in range(planes):
            fresh = 0
            for g in range(groups):
                fresh = fresh + jnp.take(received[d], (source + g) * cap + safe, axis=0)
            old = jnp.zeros_like(fresh) if picked is None else picked
            picked = jnp.where((valid & (own_plane % planes == d))[:, :, None, None], fresh, old)
        return picked

    masked = jnp.where(own_live[:, None, None], footprints, jnp.zeros_like(footprints))
    halves = masked.reshape(slots, SPAN, 2, 2, VOX)
    by_block = lambda part: jnp.transpose(part, (1, 2, 0, 3)).reshape(-1, VOX)
    top = by_block(halves[:, :, 0])
    bottom = by_block(halves[:, :, 1])
    above = lax.ppermute(bottom, "tile", ups)
    below = lax.ppermute(top, "tile", downs)
    own_traces = traces[0]
    trace_above = lax.ppermute(own_traces, "tile", ups)
    trace_below = lax.ppermute(own_traces, "tile", downs)
    cols = jnp.concatenate([jnp.transpose(masked, (1, 0, 2)).reshape(-1, VOX), above, below], axis=0)

    def edge_ids(neighbour, d, row, shift):
        base_there = lax.dynamic_index_in_dim(base, jnp.clip(neighbour, 0, tiles - 1), 0, False)
        row_there = (base_there // xb) % rb + d
        steps = (jnp.arange(SPAN)[:, None] * rb * xb + d * xb + jnp.arange(2)).reshape(-1, 1).astype(jnp.int32)
        good = (row_there == row) & (neighbour >= 0) & (neighbour < tiles)
        return jnp.where(good, base_there + steps + shift, -1).reshape(-1)

    col_ids = jnp.concatenate(
        [blocks.T.reshape(-1), edge_ids(me - 1, 1, pb, -pb * xb), edge_ids(me + 1, 0, 0, pb * xb)]
    )[None]
    own_ids = blocks.T[:, :, None]
    own_flat = masked.reshape(slots, NB * VOX)

    def columns(own, up, down):
        return jnp.concatenate([jnp.tile(own, (NB, 1)), jnp.tile(up, (NB // 2, 1)), jnp.tile(down, (NB // 2, 1))])

    wide = lambda part: jnp.repeat(part, LANES // fh, axis=1)
    denom_c = overlaps(
        own_flat, own_ids, cols, col_ids, columns(wide(own_traces), wide(trace_above), wide(trace_below))
    )

    picked = one_round(0, None)
    _, picked = lax.while_loop(
        lambda state: state[0] < rounds,
        lambda state: (state[0] + 1, one_round(state[0], state[1])),
        (jnp.int32(1), picked),
    )
    new_wide, numer = update(
        picked.reshape(-1, LANES), masked.reshape(slots * SPAN * 2, 2 * VOX), wide(own_traces), denom_c
    )
    new = new_wide[:, :: LANES // fh]

    near, numer_other = exchange(new_wide, numer, tiles)
    new_footprints = finish(
        own_flat, own_ids, cols, col_ids, new_wide, near[0],
        columns(new_wide, near[1], near[3]), columns(near[0], near[2], near[4]),
        numer.reshape(slots, NB * VOX), numer_other.reshape(slots, NB * VOX),
    )
    return (new[None], new_footprints.reshape(slots, NB, VOX))


def solution(mesh):
    placed = (
        P("nrn", "tile", None, None),
        P("nrn", "tile", None),
        P("tile", None, None),
        P("tile", None),
        P("nrn", "tile", None),
        P("tile"),
    )
    return jax.shard_map(
        shards,
        mesh=mesh,
        in_specs=placed,
        out_specs=(P("nrn", "tile", None), P("tile", None, None)),
        check_vma=False,
    )
```

```python
import functools

import jax
import jax.numpy as jnp
from jax import lax
from jax.experimental import pallas as pl
from jax.experimental.pallas import tpu as pltpu
from jax.sharding import PartitionSpec as P

Z = 32
PR = 8
PC = 16
VOX = 128
NB = 16
SPAN = 4
LANES = 128
WIN_R = 2 * PR
WIN_C = 2 * PC
EPSILON = 1e-06
MIB = 1 << 20
EXACT = lax.Precision.HIGHEST


def extract_kernel(
    cap, step, tiles, plane, frames, height, width,
    rows_ref, cols_ref, counts_ref, shift_ref, group_ref, movie_ref, out_ref, scr,
):
    frame = pl.program_id(0)

    scr[frame, pl.ds(0, 8), :] = jnp.zeros((8, width + 256), jnp.float32)
    scr[frame, pl.ds(height + 8, 16), :] = jnp.zeros((16, width + 256), jnp.float32)

    @pl.loop(0, height // 32)
    def _(i):
        at = pl.ds(pl.multiple_of(i * 32 + 8, 8), 32)
        scr[frame, at, pl.ds(0, 128)] = jnp.zeros((32, 128), jnp.float32)
        scr[frame, at, pl.ds(width + 128, 128)] = jnp.zeros((32, 128), jnp.float32)
        part = movie_ref[0, pl.ds(pl.multiple_of(i * 32, 32), 32), :]
        scr[frame, at, pl.ds(128, width)] = part.astype(jnp.float32)

    @pl.when(frame == frames - 1)
    def _():
        out_ref[...] = jnp.zeros_like(out_ref)
        lane = lax.broadcasted_iota(jnp.int32, (WIN_R + 8, LANES), 1)
        row = lax.broadcasted_iota(jnp.int32, (WIN_R, LANES), 0)
        first = group_ref[0] * frames
        moves = [
            (shift_ref[2 * (plane * frames + f)], shift_ref[2 * (plane * frames + f) + 1]) for f in range(frames)
        ]

        def one(slot):
            r0 = rows_ref[slot]
            c0 = cols_ref[slot]
            window = jnp.zeros((WIN_R, LANES), jnp.float32)
            for f in range(frames):
                down, right = moves[f]
                top = r0 - down + 8
                left = c0 - right + 128
                m = lax.shift_right_logical(left, 7)
                o = left - m * 128
                k = top & 7
                at = pl.ds(pl.multiple_of(top - k, 8), WIN_R + 8)
                near = scr[f, at, pl.ds(pl.multiple_of(m * 128, 128), 128)]
                far = scr[f, at, pl.ds(pl.multiple_of(m * 128 + 128, 128), 128)]
                place = (first + f) * WIN_C
                both = jnp.where(lane >= o, near, far)
                parts = []
                for i in range(0, WIN_R, 8):
                    part = jnp.where(row[:8] >= k, both[i : i + 8], both[i + 8 : i + 16])
                    part = pltpu.roll(part, (8 - k) & 7, 0)
                    parts.append(pltpu.roll(part, (place - o + 128) & 127, 1))
                both = jnp.concatenate(parts, axis=0)
                window = jnp.where((lane[:WIN_R] >= place) & (lane[:WIN_R] < place + WIN_C), both, window)
            return jnp.where(row + r0 < height, window, 0.0).astype(jnp.bfloat16)

        @pl.loop(0, tiles)
        def _(t):
            def some(i, carry):
                slots = [t * cap + i * step + j for j in range(step)]
                windows = [one(slot) for slot in slots]
                for slot, window in zip(slots, windows):
                    out_ref[slot] = window
                return carry

            lax.fori_loop(0, (counts_ref[t] + step - 1) // step, some, 0)


def extract(movie, shifts, rows, cols, counts, group, cap, step, tiles, plane, frames):
    _, height, width = movie.shape
    smem = pl.BlockSpec(memory_space=pltpu.SMEM)
    return pl.pallas_call(
        functools.partial(extract_kernel, cap, step, tiles, plane, frames, height, width),
        grid=(frames,),
        in_specs=[smem] * 5 + [pl.BlockSpec((1, height, width), lambda f: (plane * frames + f, 0, 0))],
        out_specs=pl.BlockSpec((tiles * cap, WIN_R, LANES), lambda f: (0, 0, 0)),
        out_shape=jax.ShapeDtypeStruct((tiles * cap, WIN_R, LANES), jnp.bfloat16),
        scratch_shapes=[pltpu.VMEM((frames, height + 24, width + 256), jnp.float32)],
        compiler_params=pltpu.CompilerParams(vmem_limit_bytes=56 * MIB),
        name="extract_windows",
    )(rows.reshape(-1), cols.reshape(-1), counts, shifts.reshape(-1), group.reshape(1), movie)


def exchange_kernel(tiles, new_ref, numer_ref, near_ref, other_ref, send_sem, recv_sem):
    t, p = lax.axis_index("tile"), lax.axis_index("nrn")
    q = 1 - p
    has_above, has_below = t > 0, t < tiles - 1
    mesh_id = pl.DeviceIdType.MESH
    barrier = pltpu.get_barrier_semaphore()
    pl.semaphore_signal(barrier, inc=1, device_id=(t, q), device_id_type=mesh_id)

    @pl.when(has_above)
    def _():
        for peer in (p, q):
            pl.semaphore_signal(barrier, inc=1, device_id=(t - 1, peer), device_id_type=mesh_id)

    @pl.when(has_below)
    def _():
        for peer in (p, q):
            pl.semaphore_signal(barrier, inc=1, device_id=(t + 1, peer), device_id_type=mesh_id)

    pl.semaphore_wait(barrier, 1 + 2 * has_above.astype(jnp.int32) + 2 * has_below.astype(jnp.int32))

    def copy(src, dst, i, to):
        return pltpu.make_async_remote_copy(
            src_ref=src, dst_ref=dst, send_sem=send_sem.at[i], recv_sem=recv_sem.at[i],
            device_id=to, device_id_type=mesh_id,
        )

    partner = copy(new_ref, near_ref.at[0], 0, (t, q))
    large = copy(numer_ref, other_ref, 5, (t, q))
    to_below = [copy(new_ref, near_ref.at[1 + i], 1 + i, (t + 1, peer)) for i, peer in enumerate((p, q))]
    to_above = [copy(new_ref, near_ref.at[3 + i], 3 + i, (t - 1, peer)) for i, peer in enumerate((p, q))]

    @pl.when(has_below)
    def _():
        for one in to_below:
            one.start()

    @pl.when(has_above)
    def _():
        for one in to_above:
            one.start()

    partner.start()
    large.start()

    @pl.when(has_below)
    def _():
        for one in to_below:
            one.wait_send()
        for one in to_above:
            one.wait_recv()

    @pl.when(has_above)
    def _():
        for one in to_above:
            one.wait_send()
        for one in to_below:
            one.wait_recv()

    partner.wait()
    large.wait()


def exchange(new, numer, tiles):
    anywhere = pl.BlockSpec(memory_space=pl.ANY)
    return pl.pallas_call(
        functools.partial(exchange_kernel, tiles),
        in_specs=[anywhere, anywhere],
        out_specs=[anywhere, anywhere],
        out_shape=[
            jax.ShapeDtypeStruct((5,) + new.shape, jnp.float32),
            jax.ShapeDtypeStruct(numer.shape, jnp.float32),
        ],
        scratch_shapes=[pltpu.SemaphoreType.DMA((6,)), pltpu.SemaphoreType.DMA((6,))],
        compiler_params=pltpu.CompilerParams(collective_id=0, has_side_effects=True),
        name="exchange",
    )(new, numer)


def overlap_kernel(own_ref, own_ids_ref, cols_ref, col_ids_ref, traces_ref, out_ref, acc):
    b = pl.program_id(0)
    products = lax.dot_general(
        own_ref[...], cols_ref[...], (((1,), (1,)), ((), ())), preferred_element_type=jnp.float32
    )
    kept = jnp.where(own_ids_ref[0] == col_ids_ref[...], products, 0.0)

    @pl.when(b == 0)
    def _():
        acc[...] = kept

    @pl.when(b > 0)
    def _():
        acc[...] += kept

    @pl.when(b == pl.num_programs(0) - 1)
    def _():
        out_ref[...] = (
            jnp.dot(acc[...], traces_ref[...], precision=EXACT, preferred_element_type=jnp.float32) + EPSILON
        )


def whole_spec(shape):
    return pl.BlockSpec(shape, lambda i: (0,) * len(shape))


def overlaps(own, own_ids, cols, col_ids, col_traces):
    slots = own.shape[0]
    width = cols.shape[0]
    return pl.pallas_call(
        overlap_kernel,
        grid=(NB,),
        in_specs=[
            pl.BlockSpec((slots, VOX), lambda b: (0, b)),
            pl.BlockSpec((1, slots, 1), lambda b: (b, 0, 0)),
            whole_spec(cols.shape),
            whole_spec(col_ids.shape),
            whole_spec(col_traces.shape),
        ],
        out_specs=whole_spec((slots, LANES)),
        out_shape=jax.ShapeDtypeStruct((slots, LANES), jnp.float32),
        scratch_shapes=[pltpu.VMEM((slots, width), jnp.float32)],
        compiler_params=pltpu.CompilerParams(vmem_limit_bytes=32 * MIB),
        name="denom_c",
    )(own, own_ids, cols, col_ids, col_traces)


def row_keeper(pairs):
    lane = lax.broadcasted_iota(jnp.int32, (pairs, PR, 2 * VOX), 2)
    row = lax.broadcasted_iota(jnp.int32, (pairs, PR, 2 * VOX), 1)
    return (lane & (VOX - 1)) // PC == row


def fold_matrix():
    out_lane = lax.broadcasted_iota(jnp.int32, (LANES, 2 * VOX), 1)
    in_lane = lax.broadcasted_iota(jnp.int32, (LANES, 2 * VOX), 0)
    return ((in_lane & (WIN_C - 1)) == (out_lane // VOX) * PC + (out_lane & (PC - 1))).astype(jnp.bfloat16)


def feet_kernel(masked_ref, out_ref):
    pairs = masked_ref.shape[0]
    feet = masked_ref[...].astype(jnp.float32)
    feet = jnp.where(row_keeper(pairs), feet[:, None, :], 0.0).reshape(pairs * PR, 2 * VOX).astype(jnp.bfloat16)
    feet = lax.dot_general(feet, fold_matrix(), (((1,), (1,)), ((), ())), preferred_element_type=jnp.float32)
    out_ref[...] = feet.astype(jnp.bfloat16)


def window_feet(masked):
    total = masked.shape[0]
    pairs = total // 4
    return pl.pallas_call(
        feet_kernel,
        grid=(4,),
        in_specs=[pl.BlockSpec((pairs, 2 * VOX), lambda i: (i, 0))],
        out_specs=pl.BlockSpec((pairs * PR, LANES), lambda i: (i, 0)),
        out_shape=jax.ShapeDtypeStruct((total * PR, LANES), jnp.bfloat16),
        compiler_params=pltpu.CompilerParams(vmem_limit_bytes=32 * MIB),
        name="window_feet",
    )(masked)


def update_kernel(
    cap, groups, planes, index_ref, feet_ref, extra_ref, traces_ref, denom_ref, *refs
):
    received, (new_ref, numer_ref, windows) = refs[:planes], refs[planes:]
    slots = traces_ref.shape[0]
    count = slots * SPAN
    pairs = count * 2
    length = received[0].shape[0]
    first = pl.program_id(0) * count
    for w in range(count):
        index = index_ref[first + w]
        window = extra_ref[w].astype(jnp.float32)
        for d in range(planes):
            at = jnp.clip(index - d * length, 0, length - 1 - (groups - 1) * cap)
            got = received[d][at].astype(jnp.float32)
            for g in range(1, groups):
                got += received[d][at + g * cap].astype(jnp.float32)
            window = jnp.where(index >= d * length, got, window)
        windows[pl.ds(w * WIN_R, WIN_R), :] = window

    group_a = lax.broadcasted_iota(jnp.int32, (LANES, LANES), 0) // WIN_C
    group_b = lax.broadcasted_iota(jnp.int32, (LANES, LANES), 1) // WIN_C
    group_sum = (group_a == group_b).astype(jnp.float32)
    fold = fold_matrix()
    seen = windows[...]
    sums = (feet_ref[...].astype(jnp.float32) * seen).reshape(slots, SPAN * WIN_R, LANES).sum(axis=1)
    numer_c = jnp.dot(sums, group_sum, precision=EXACT, preferred_element_type=jnp.float32)
    new = traces_ref[...] * numer_c / denom_ref[...]
    new_ref[...] = new
    scaled = (seen.reshape(slots, SPAN * WIN_R, LANES) * new[:, None, :]).reshape(pairs * PR, LANES)
    high = scaled.astype(jnp.bfloat16)
    low = (scaled - high.astype(jnp.float32)).astype(jnp.bfloat16)
    spread = jnp.dot(high, fold, preferred_element_type=jnp.float32)
    spread += jnp.dot(low, fold, preferred_element_type=jnp.float32)
    numer = jnp.where(row_keeper(pairs), spread.reshape(pairs, PR, 2 * VOX), 0.0).sum(axis=1)
    for e in range(2):
        numer_ref[e] = numer[:, e * VOX : (e + 1) * VOX]


def update(index, feet, extra, traces, denom, received, cap, groups):
    slots = traces.shape[0]
    step = 24
    pairs = step * SPAN * 2
    trace_spec = pl.BlockSpec((step, LANES), lambda i: (i, 0))
    numer_spec = pl.BlockSpec((2, pairs, VOX), lambda i: (0, i, 0))
    return pl.pallas_call(
        functools.partial(update_kernel, cap, groups, len(received)),
        grid=(slots // step,),
        in_specs=[
            pl.BlockSpec(memory_space=pltpu.SMEM),
            pl.BlockSpec((pairs * PR, LANES), lambda i: (i, 0)),
            pl.BlockSpec((step * SPAN, WIN_R, LANES), lambda i: (i, 0, 0)),
            trace_spec,
            trace_spec,
        ]
        + [whole_spec(part.shape) for part in received],
        out_specs=[trace_spec, numer_spec],
        out_shape=[
            jax.ShapeDtypeStruct((slots, LANES), jnp.float32),
            jax.ShapeDtypeStruct((2, slots * SPAN * 2, VOX), jnp.float32),
        ],
        scratch_shapes=[pltpu.VMEM((pairs * PR, LANES), jnp.float32)],
        compiler_params=pltpu.CompilerParams(vmem_limit_bytes=48 * MIB),
        name="update_traces",
    )(index, feet, extra, traces, denom, *received)


def finish_kernel(
    own_ref, own_ids_ref, cols_ref, col_ids_ref, new_ref, near_ref, mine_ref, other_ref, out_ref, pair
):
    j = pl.program_id(0)
    slots = new_ref.shape[0]

    @pl.when(j == 0)
    def _():
        def products(own, up, down):
            columns = jnp.concatenate([own] * NB + [up] * (NB // 2) + [down] * (NB // 2), axis=0)
            return lax.dot_general(
                own, columns, (((1,), (1,)), ((), ())), precision=EXACT, preferred_element_type=jnp.float32
            )

        both = products(new_ref[...], near_ref[1], near_ref[3])
        both += products(near_ref[0], near_ref[2], near_ref[4])
        pair[...] = both * (1.0 / WIN_C)

    highs, lows = [], []
    for e in range(2):
        weight = jnp.where(own_ids_ref[e] == col_ids_ref[...], pair[...], 0.0)
        highs.append(weight.astype(jnp.bfloat16))
        lows.append((weight - highs[-1].astype(jnp.float32)).astype(jnp.bfloat16))
    sums = jnp.dot(jnp.concatenate(highs + lows, axis=0), cols_ref[...], preferred_element_type=jnp.float32)
    for e in range(2):
        denom = sums[e * slots : (e + 1) * slots] + sums[(e + 2) * slots : (e + 3) * slots]
        at = pl.ds(e * slots * (NB // 2) + j, slots, stride=NB // 2)
        numer = mine_ref[at, :] + other_ref[at, :]
        lanes = pl.ds(e * VOX, VOX)
        out_ref[:, lanes] = (own_ref[:, lanes].astype(jnp.float32) * numer / (denom + EPSILON)).astype(jnp.bfloat16)


def finish(own, own_ids, cols, col_ids, new, near, mine, other):
    slots = own.shape[0]
    width = cols.shape[0]
    block = pl.BlockSpec((slots, 2 * VOX), lambda j: (0, j))
    return pl.pallas_call(
        finish_kernel,
        grid=(NB // 2,),
        in_specs=[block, pl.BlockSpec((2, slots, 1), lambda j: (j, 0, 0))]
        + [whole_spec(part.shape) for part in (cols, col_ids, new, near, mine, other)],
        out_specs=block,
        out_shape=jax.ShapeDtypeStruct((slots, NB * VOX), jnp.bfloat16),
        scratch_shapes=[pltpu.VMEM((slots, width), jnp.float32)],
        compiler_params=pltpu.CompilerParams(vmem_limit_bytes=48 * MIB),
        name="new_footprints",
    )(own, own_ids, cols, col_ids, new, near, mine, other)


def shards(movie, shifts, footprints, blocks, traces, counts):
    images, height, width = movie.shape[1:]
    tiles, me = lax.axis_size("tile"), lax.axis_index("tile")
    band = height // tiles
    pb = band // PR
    rb, xb = pb + 1, width // PC
    fh, slots = traces.shape[2], footprints.shape[0]
    frames = min(images, fh)
    planes = images // frames
    groups = fh // frames
    cap, step = 25, 5
    ups = [(i, i + 1) for i in range(tiles - 1)]
    downs = [(i + 1, i) for i in range(tiles - 1)]

    own_traces = traces[0]
    numbers = jnp.concatenate([blocks[:, 0], counts]).astype(jnp.float32)
    info = lax.all_gather(jnp.concatenate([numbers, own_traces.reshape(-1)]), "tile")
    base, live_count = info[:, :slots].astype(jnp.int32), info[:, slots : slots + 1].astype(jnp.int32)
    all_traces = info[:, slots + 1 :].reshape(tiles, slots, fh)
    z, r, x = base // (rb * xb), (base // xb) % rb, base % xb
    live = jnp.arange(slots, dtype=jnp.int32) < live_count
    plane_ids = jnp.arange(Z, dtype=jnp.int32)
    cover = live[:, None, :] & (z[:, None, :] <= plane_ids[:, None]) & (plane_ids[:, None] < z[:, None, :] + SPAN)
    before = jnp.triu(jnp.ones((slots, slots), jnp.bfloat16), 1)
    rank = jnp.einsum(
        "tzk,kj->tzj", cover.astype(jnp.bfloat16), before, preferred_element_type=jnp.float32
    ).astype(jnp.int32)
    totals = cover.sum(axis=2, dtype=jnp.int32)
    rounds = (jnp.max(totals) + cap - 1) // cap

    first_plane = (me // groups) * planes
    my_place = lax.dynamic_slice_in_dim(jnp.where(cover, rank, -1), first_plane, planes, 1)
    my_totals = lax.dynamic_slice_in_dim(totals, first_plane, planes, 1)
    row_start = jnp.arange(tiles, dtype=jnp.int32)[:, None] * band + PR * r
    col_start = PC * x
    own_z = blocks[:, 0] // (rb * xb)
    own_live = jnp.arange(slots, dtype=jnp.int32) < counts[0]
    own_plane = own_z[:, None] + jnp.arange(SPAN, dtype=jnp.int32)
    own_place = lax.dynamic_index_in_dim(rank, me, 0, False)
    own_place = jnp.where(own_plane[:, :, None] == plane_ids, own_place.T[:, None, :], 0).sum(axis=2)
    source = (own_plane // planes) * groups

    def one_round(number):
        offset = number * cap
        slot_ids = jnp.arange(cap, dtype=jnp.int32) + offset
        hit = my_place[:, :, None] == slot_ids[:, None]
        rows = jnp.where(hit, row_start[:, None, None, :], 0).sum(axis=3)
        cols = jnp.where(hit, col_start[:, None, None, :], 0).sum(axis=3)
        limits = jnp.clip(my_totals - offset, 0, cap)
        received = []
        for d in range(planes):
            sent = extract(
                movie[0], shifts[0], rows[:, d], cols[:, d], limits[:, d], me % groups, cap, step, tiles, d, frames
            )
            received.append(lax.all_to_all(sent, "tile", split_axis=0, concat_axis=0, tiled=True))
        local = own_place - offset
        valid = own_live[:, None] & (local >= 0) & (local < cap)
        index = source * cap + jnp.clip(local, 0, cap - 1)
        return received, index, valid

    def later_round(state):
        number, picked = state
        received, index, valid = one_round(number)
        for d in range(planes):
            fresh = 0
            for g in range(groups):
                fresh = fresh + jnp.take(received[d], index + g * cap, axis=0)
            picked = jnp.where((valid & (own_plane % planes == d))[:, :, None, None], fresh, picked)
        return number + 1, picked

    masked = jnp.where(own_live[:, None, None], footprints, jnp.zeros_like(footprints))
    halves = masked.reshape(slots, SPAN, 2, 2, VOX)
    by_block = lambda part: jnp.transpose(part, (1, 2, 0, 3)).reshape(-1, VOX)
    top = by_block(halves[:, :, 0])
    bottom = by_block(halves[:, :, 1])
    above = lax.ppermute(bottom, "tile", ups)
    below = lax.ppermute(top, "tile", downs)
    trace_above = lax.dynamic_index_in_dim(all_traces, jnp.maximum(me - 1, 0), 0, False)
    trace_below = lax.dynamic_index_in_dim(all_traces, jnp.minimum(me + 1, tiles - 1), 0, False)
    cols = jnp.concatenate([jnp.transpose(masked, (1, 0, 2)).reshape(-1, VOX), above, below], axis=0)

    def edge_ids(neighbour, d, row, shift):
        base_there = lax.dynamic_index_in_dim(base, jnp.clip(neighbour, 0, tiles - 1), 0, False)
        row_there = (base_there // xb) % rb + d
        steps = (jnp.arange(SPAN)[:, None] * rb * xb + d * xb + jnp.arange(2)).reshape(-1, 1).astype(jnp.int32)
        good = (row_there == row) & (neighbour >= 0) & (neighbour < tiles)
        return jnp.where(good, base_there + steps + shift, -1).reshape(-1)

    col_ids = jnp.concatenate(
        [blocks.T.reshape(-1), edge_ids(me - 1, 1, pb, -pb * xb), edge_ids(me + 1, 0, 0, pb * xb)]
    )[None]
    own_ids = blocks.T[:, :, None]
    own_flat = masked.reshape(slots, NB * VOX)

    def columns(own, up, down):
        return jnp.concatenate([jnp.tile(own, (NB, 1)), jnp.tile(up, (NB // 2, 1)), jnp.tile(down, (NB // 2, 1))])

    wide = lambda part: jnp.repeat(part, LANES // fh, axis=1)
    denom_c = overlaps(
        own_flat, own_ids, cols, col_ids, columns(wide(own_traces), wide(trace_above), wide(trace_below))
    )

    pair_feet = masked.reshape(slots * SPAN * 2, 2 * VOX)
    feet = window_feet(pair_feet)
    received, index, valid = one_round(0)
    index = jnp.where(valid, index + (own_plane % planes) * (tiles * cap), -1).reshape(-1)
    _, later = lax.while_loop(
        lambda state: state[0] < rounds,
        later_round,
        (jnp.int32(1), jnp.zeros((slots, SPAN, WIN_R, LANES), jnp.bfloat16)),
    )
    new_wide, numer = update(
        index, feet, later.reshape(-1, WIN_R, LANES), wide(own_traces), denom_c, received, cap, groups
    )
    new = new_wide[:, :: LANES // fh]

    numer = numer.reshape(-1, VOX)
    near, numer_other = exchange(new_wide, numer, tiles)
    new_footprints = finish(own_flat, own_ids, cols, col_ids, new_wide, near, numer, numer_other)
    return (new[None], new_footprints.reshape(slots, NB, VOX))


def solution(mesh):
    placed = (
        P("nrn", "tile", None, None),
        P("nrn", "tile", None),
        P("tile", None, None),
        P("tile", None),
        P("nrn", "tile", None),
        P("tile"),
    )
    return jax.shard_map(
        shards,
        mesh=mesh,
        in_specs=placed,
        out_specs=(P("nrn", "tile", None), P("tile", None, None)),
        check_vma=False,
    )
```

```python
import functools

import jax
import jax.numpy as jnp
from jax import lax
from jax.experimental import pallas as pl
from jax.experimental.pallas import tpu as pltpu
from jax.sharding import PartitionSpec as P

Z = 32
PR = 8
PC = 16
VOX = 128
NB = 16
SPAN = 4
LANES = 128
WIN_R = 2 * PR
WIN_C = 2 * PC
EPSILON = 1e-06
MIB = 1 << 20
EXACT = lax.Precision.HIGHEST


def extract_kernel(
    cap, step, tiles, plane, frames, height, width,
    rows_ref, cols_ref, counts_ref, shift_ref, group_ref, movie_ref, out_ref, scr,
):
    frame = pl.program_id(0)

    scr[frame, pl.ds(0, 8), :] = jnp.zeros((8, width + 256), jnp.float32)
    scr[frame, pl.ds(height + 8, 16), :] = jnp.zeros((16, width + 256), jnp.float32)

    @pl.loop(0, height // 32)
    def _(i):
        at = pl.ds(pl.multiple_of(i * 32 + 8, 8), 32)
        scr[frame, at, pl.ds(0, 128)] = jnp.zeros((32, 128), jnp.float32)
        scr[frame, at, pl.ds(width + 128, 128)] = jnp.zeros((32, 128), jnp.float32)
        part = movie_ref[0, pl.ds(pl.multiple_of(i * 32, 32), 32), :]
        scr[frame, at, pl.ds(128, width)] = part.astype(jnp.float32)

    @pl.when(frame == frames - 1)
    def _():
        out_ref[...] = jnp.zeros_like(out_ref)
        lane = lax.broadcasted_iota(jnp.int32, (WIN_R + 8, LANES), 1)
        row = lax.broadcasted_iota(jnp.int32, (WIN_R, LANES), 0)
        first = group_ref[0] * frames
        moves = [
            (shift_ref[2 * (plane * frames + f)], shift_ref[2 * (plane * frames + f) + 1]) for f in range(frames)
        ]

        def one(slot):
            r0 = rows_ref[slot]
            c0 = cols_ref[slot]
            window = jnp.zeros((WIN_R, LANES), jnp.float32)
            for f in range(frames):
                down, right = moves[f]
                top = r0 - down + 8
                left = c0 - right + 128
                m = lax.shift_right_logical(left, 7)
                o = left - m * 128
                k = top & 7
                at = pl.ds(pl.multiple_of(top - k, 8), WIN_R + 8)
                near = scr[f, at, pl.ds(pl.multiple_of(m * 128, 128), 128)]
                far = scr[f, at, pl.ds(pl.multiple_of(m * 128 + 128, 128), 128)]
                place = (first + f) * WIN_C
                both = jnp.where(lane >= o, near, far)
                parts = []
                for i in range(0, WIN_R, 8):
                    part = jnp.where(row[:8] >= k, both[i : i + 8], both[i + 8 : i + 16])
                    part = pltpu.roll(part, (8 - k) & 7, 0)
                    parts.append(pltpu.roll(part, (place - o + 128) & 127, 1))
                both = jnp.concatenate(parts, axis=0)
                window = jnp.where((lane[:WIN_R] >= place) & (lane[:WIN_R] < place + WIN_C), both, window)
            return jnp.where(row + r0 < height, window, 0.0).astype(jnp.bfloat16)

        @pl.loop(0, tiles)
        def _(t):
            def some(i, carry):
                slots = [t * cap + i * step + j for j in range(step)]
                windows = [one(slot) for slot in slots]
                for slot, window in zip(slots, windows):
                    out_ref[slot] = window
                return carry

            lax.fori_loop(0, (counts_ref[t] + step - 1) // step, some, 0)


def extract(movie, shifts, rows, cols, counts, group, cap, step, tiles, plane, frames):
    _, height, width = movie.shape
    smem = pl.BlockSpec(memory_space=pltpu.SMEM)
    return pl.pallas_call(
        functools.partial(extract_kernel, cap, step, tiles, plane, frames, height, width),
        grid=(frames,),
        in_specs=[smem] * 5 + [pl.BlockSpec((1, height, width), lambda f: (plane * frames + f, 0, 0))],
        out_specs=pl.BlockSpec((tiles * cap, WIN_R, LANES), lambda f: (0, 0, 0)),
        out_shape=jax.ShapeDtypeStruct((tiles * cap, WIN_R, LANES), jnp.bfloat16),
        scratch_shapes=[pltpu.VMEM((frames, height + 24, width + 256), jnp.float32)],
        compiler_params=pltpu.CompilerParams(vmem_limit_bytes=56 * MIB),
        name="extract_windows",
    )(rows.reshape(-1), cols.reshape(-1), counts, shifts.reshape(-1), group.reshape(1), movie)


def gather_kernel(tiles, own_ref, all_ref, send_sem, recv_sem, own_sem):
    t, p = lax.axis_index("tile"), lax.axis_index("nrn")
    mesh_id = pl.DeviceIdType.MESH
    barrier = pltpu.get_barrier_semaphore()

    def peer(i):
        return lax.rem(t + i, tiles)

    @pl.loop(1, tiles)
    def _(i):
        pl.semaphore_signal(barrier, inc=1, device_id=(peer(i), p), device_id_type=mesh_id)

    pl.semaphore_wait(barrier, tiles - 1)

    def copy(i, slot):
        return pltpu.make_async_remote_copy(
            src_ref=own_ref, dst_ref=all_ref.at[slot], send_sem=send_sem.at[i], recv_sem=recv_sem.at[i],
            device_id=(peer(i), p), device_id_type=mesh_id,
        )

    @pl.loop(1, tiles)
    def _(i):
        copy(i, t).start()

    own = pltpu.make_async_copy(own_ref, all_ref.at[t], own_sem)
    own.start()
    own.wait()

    @pl.loop(1, tiles)
    def _(i):
        copy(i, t).wait_send()
        copy(i, lax.rem(t + tiles - i, tiles)).wait_recv()


def gather(own, tiles):
    vmem = pl.BlockSpec(memory_space=pltpu.VMEM)
    return pl.pallas_call(
        functools.partial(gather_kernel, tiles),
        in_specs=[vmem],
        out_specs=vmem,
        out_shape=jax.ShapeDtypeStruct((tiles,) + own.shape, own.dtype),
        scratch_shapes=[
            pltpu.SemaphoreType.DMA((tiles,)), pltpu.SemaphoreType.DMA((tiles,)), pltpu.SemaphoreType.DMA,
        ],
        compiler_params=pltpu.CompilerParams(collective_id=0, has_side_effects=True),
        name="gather_numbers",
    )(own)


def overlap_kernel(own_ref, own_ids_ref, cols_ref, col_ids_ref, traces_ref, out_ref, acc):
    b = pl.program_id(0)
    products = lax.dot_general(
        own_ref[...], cols_ref[...], (((1,), (1,)), ((), ())), preferred_element_type=jnp.float32
    )
    kept = jnp.where(own_ids_ref[0] == col_ids_ref[...], products, 0.0)

    @pl.when(b == 0)
    def _():
        acc[...] = kept

    @pl.when(b > 0)
    def _():
        acc[...] += kept

    @pl.when(b == pl.num_programs(0) - 1)
    def _():
        out_ref[...] = (
            jnp.dot(acc[...], traces_ref[...], precision=EXACT, preferred_element_type=jnp.float32) + EPSILON
        )


def whole_spec(shape):
    return pl.BlockSpec(shape, lambda i: (0,) * len(shape))


def overlaps(own, own_ids, cols, col_ids, col_traces):
    slots = own.shape[0]
    width = cols.shape[0]
    return pl.pallas_call(
        overlap_kernel,
        grid=(NB,),
        in_specs=[
            pl.BlockSpec((slots, VOX), lambda b: (0, b)),
            pl.BlockSpec((1, slots, 1), lambda b: (b, 0, 0)),
            whole_spec(cols.shape),
            whole_spec(col_ids.shape),
            whole_spec(col_traces.shape),
        ],
        out_specs=whole_spec((slots, LANES)),
        out_shape=jax.ShapeDtypeStruct((slots, LANES), jnp.float32),
        scratch_shapes=[pltpu.VMEM((slots, width), jnp.float32)],
        compiler_params=pltpu.CompilerParams(vmem_limit_bytes=32 * MIB),
        name="denom_c",
    )(own, own_ids, cols, col_ids, col_traces)


def row_keeper(pairs):
    lane = lax.broadcasted_iota(jnp.int32, (pairs, PR, 2 * VOX), 2)
    row = lax.broadcasted_iota(jnp.int32, (pairs, PR, 2 * VOX), 1)
    return (lane & (VOX - 1)) // PC == row


def fold_matrix():
    out_lane = lax.broadcasted_iota(jnp.int32, (LANES, 2 * VOX), 1)
    in_lane = lax.broadcasted_iota(jnp.int32, (LANES, 2 * VOX), 0)
    return ((in_lane & (WIN_C - 1)) == (out_lane // VOX) * PC + (out_lane & (PC - 1))).astype(jnp.bfloat16)


def feet_kernel(masked_ref, out_ref):
    pairs = masked_ref.shape[0]
    feet = masked_ref[...].astype(jnp.float32)
    feet = jnp.where(row_keeper(pairs), feet[:, None, :], 0.0).reshape(pairs * PR, 2 * VOX).astype(jnp.bfloat16)
    feet = lax.dot_general(feet, fold_matrix(), (((1,), (1,)), ((), ())), preferred_element_type=jnp.float32)
    out_ref[...] = feet.astype(jnp.bfloat16)


def window_feet(masked):
    total = masked.shape[0]
    pairs = total // 4
    return pl.pallas_call(
        feet_kernel,
        grid=(4,),
        in_specs=[pl.BlockSpec((pairs, 2 * VOX), lambda i: (i, 0))],
        out_specs=pl.BlockSpec((pairs * PR, LANES), lambda i: (i, 0)),
        out_shape=jax.ShapeDtypeStruct((total * PR, LANES), jnp.bfloat16),
        compiler_params=pltpu.CompilerParams(vmem_limit_bytes=32 * MIB),
        name="window_feet",
    )(masked)


def update_kernel(
    cap, groups, planes, index_ref, feet_ref, extra_ref, traces_ref, denom_ref, *refs
):
    received, (new_ref, numer_ref, windows) = refs[:planes], refs[planes:]
    slots = traces_ref.shape[0]
    count = slots * SPAN
    pairs = count * 2
    length = received[0].shape[0]
    first = pl.program_id(0) * count
    for w in range(count):
        index = index_ref[first + w]
        window = extra_ref[w].astype(jnp.float32)
        for d in range(planes):
            at = jnp.clip(index - d * length, 0, length - 1 - (groups - 1) * cap)
            got = received[d][at].astype(jnp.float32)
            for g in range(1, groups):
                got += received[d][at + g * cap].astype(jnp.float32)
            window = jnp.where(index >= d * length, got, window)
        windows[pl.ds(w * WIN_R, WIN_R), :] = window

    group_a = lax.broadcasted_iota(jnp.int32, (LANES, LANES), 0) // WIN_C
    group_b = lax.broadcasted_iota(jnp.int32, (LANES, LANES), 1) // WIN_C
    group_sum = (group_a == group_b).astype(jnp.float32)
    fold = fold_matrix()
    seen = windows[...]
    sums = (feet_ref[...].astype(jnp.float32) * seen).reshape(slots, SPAN * WIN_R, LANES).sum(axis=1)
    numer_c = jnp.dot(sums, group_sum, precision=EXACT, preferred_element_type=jnp.float32)
    new = traces_ref[...] * numer_c / denom_ref[...]
    new_ref[...] = new
    scaled = (seen.reshape(slots, SPAN * WIN_R, LANES) * new[:, None, :]).reshape(pairs * PR, LANES)
    high = scaled.astype(jnp.bfloat16)
    low = (scaled - high.astype(jnp.float32)).astype(jnp.bfloat16)
    spread = jnp.dot(high, fold, preferred_element_type=jnp.float32)
    spread += jnp.dot(low, fold, preferred_element_type=jnp.float32)
    numer = jnp.where(row_keeper(pairs), spread.reshape(pairs, PR, 2 * VOX), 0.0).sum(axis=1)
    for e in range(2):
        numer_ref[e] = numer[:, e * VOX : (e + 1) * VOX]


def update(index, feet, extra, traces, denom, received, cap, groups):
    slots = traces.shape[0]
    step = 24
    pairs = step * SPAN * 2
    trace_spec = pl.BlockSpec((step, LANES), lambda i: (i, 0))
    numer_spec = pl.BlockSpec((2, pairs, VOX), lambda i: (0, i, 0))
    return pl.pallas_call(
        functools.partial(update_kernel, cap, groups, len(received)),
        grid=(slots // step,),
        in_specs=[
            pl.BlockSpec(memory_space=pltpu.SMEM),
            pl.BlockSpec((pairs * PR, LANES), lambda i: (i, 0)),
            pl.BlockSpec((step * SPAN, WIN_R, LANES), lambda i: (i, 0, 0)),
            trace_spec,
            trace_spec,
        ]
        + [whole_spec(part.shape) for part in received],
        out_specs=[trace_spec, numer_spec],
        out_shape=[
            jax.ShapeDtypeStruct((slots, LANES), jnp.float32),
            jax.ShapeDtypeStruct((2, slots * SPAN * 2, VOX), jnp.float32),
        ],
        scratch_shapes=[pltpu.VMEM((pairs * PR, LANES), jnp.float32)],
        compiler_params=pltpu.CompilerParams(vmem_limit_bytes=48 * MIB),
        name="update_traces",
    )(index, feet, extra, traces, denom, *received)


def finish_kernel(
    tiles, own_ref, own_ids_ref, cols_ref, col_ids_ref, new_ref, numer_ref, out_ref,
    near_ref, other_ref, pair, send_sem, recv_sem,
):
    t, p = lax.axis_index("tile"), lax.axis_index("nrn")
    q = 1 - p
    has_above, has_below = t > 0, t < tiles - 1
    mesh_id = pl.DeviceIdType.MESH
    barrier = pltpu.get_barrier_semaphore()
    pl.semaphore_signal(barrier, inc=1, device_id=(t, q), device_id_type=mesh_id)

    @pl.when(has_above)
    def _():
        for peer in (p, q):
            pl.semaphore_signal(barrier, inc=1, device_id=(t - 1, peer), device_id_type=mesh_id)

    @pl.when(has_below)
    def _():
        for peer in (p, q):
            pl.semaphore_signal(barrier, inc=1, device_id=(t + 1, peer), device_id_type=mesh_id)

    pl.semaphore_wait(barrier, 1 + 2 * has_above.astype(jnp.int32) + 2 * has_below.astype(jnp.int32))

    def copy(src, dst, i, to):
        return pltpu.make_async_remote_copy(
            src_ref=src, dst_ref=dst, send_sem=send_sem.at[i], recv_sem=recv_sem.at[i],
            device_id=to, device_id_type=mesh_id,
        )

    partner = copy(new_ref, near_ref.at[0], 0, (t, q))
    large = copy(numer_ref, other_ref, 5, (t, q))
    to_below = [copy(new_ref, near_ref.at[1 + i], 1 + i, (t + 1, peer)) for i, peer in enumerate((p, q))]
    to_above = [copy(new_ref, near_ref.at[3 + i], 3 + i, (t - 1, peer)) for i, peer in enumerate((p, q))]

    @pl.when(has_below)
    def _():
        for one in to_below:
            one.start()

    @pl.when(has_above)
    def _():
        for one in to_above:
            one.start()

    partner.start()
    large.start()

    slots = new_ref.shape[0]

    @pl.when(has_below)
    def _():
        for one in to_above:
            one.wait_recv()

    @pl.when(has_above)
    def _():
        for one in to_below:
            one.wait_recv()

    partner.wait()

    def products(own, up, down):
        columns = jnp.concatenate([own] * NB + [up] * (NB // 2) + [down] * (NB // 2), axis=0)
        return lax.dot_general(
            own, columns, (((1,), (1,)), ((), ())), precision=EXACT, preferred_element_type=jnp.float32
        )

    both = products(new_ref[...], near_ref[1], near_ref[3])
    both += products(near_ref[0], near_ref[2], near_ref[4])
    pair[...] = both * (1.0 / WIN_C)
    large.wait()

    @pl.loop(0, NB // 2)
    def _(j):
        highs, lows = [], []
        for e in range(2):
            weight = jnp.where(own_ids_ref[2 * j + e] == col_ids_ref[...], pair[...], 0.0)
            highs.append(weight.astype(jnp.bfloat16))
            lows.append((weight - highs[-1].astype(jnp.float32)).astype(jnp.bfloat16))
        sums = jnp.dot(jnp.concatenate(highs + lows, axis=0), cols_ref[...], preferred_element_type=jnp.float32)
        for e in range(2):
            denom = sums[e * slots : (e + 1) * slots] + sums[(e + 2) * slots : (e + 3) * slots]
            at = pl.ds(e * slots * (NB // 2) + j, slots, stride=NB // 2)
            numer = numer_ref[at, :] + other_ref[at, :]
            lanes = pl.ds(pl.multiple_of((2 * j + e) * VOX, VOX), VOX)
            out_ref[:, lanes] = (own_ref[:, lanes].astype(jnp.float32) * numer / (denom + EPSILON)).astype(
                jnp.bfloat16
            )

    @pl.when(has_below)
    def _():
        for one in to_below:
            one.wait_send()

    @pl.when(has_above)
    def _():
        for one in to_above:
            one.wait_send()


def finish(own, own_ids, cols, col_ids, new, numer, tiles):
    vmem = pl.BlockSpec(memory_space=pltpu.VMEM)
    slots, width = own.shape[0], cols.shape[0]
    return pl.pallas_call(
        functools.partial(finish_kernel, tiles),
        in_specs=[vmem] * 6,
        out_specs=vmem,
        out_shape=jax.ShapeDtypeStruct(own.shape, jnp.bfloat16),
        scratch_shapes=[
            pltpu.VMEM((5,) + new.shape, jnp.float32),
            pltpu.VMEM(numer.shape, jnp.float32),
            pltpu.VMEM((slots, width), jnp.float32),
            pltpu.SemaphoreType.DMA((6,)),
            pltpu.SemaphoreType.DMA((6,)),
        ],
        compiler_params=pltpu.CompilerParams(
            collective_id=1, has_side_effects=True, vmem_limit_bytes=48 * MIB
        ),
        name="new_footprints",
    )(own, own_ids, cols, col_ids, new, numer)


def shards(movie, shifts, footprints, blocks, traces, counts):
    images, height, width = movie.shape[1:]
    tiles, me = lax.axis_size("tile"), lax.axis_index("tile")
    band = height // tiles
    pb = band // PR
    rb, xb = pb + 1, width // PC
    fh, slots = traces.shape[2], footprints.shape[0]
    frames = min(images, fh)
    planes = images // frames
    groups = fh // frames
    cap, step = 25, 5
    ups = [(i, i + 1) for i in range(tiles - 1)]
    downs = [(i + 1, i) for i in range(tiles - 1)]

    own_traces = traces[0]
    numbers = jnp.concatenate([blocks[:, 0], counts]).astype(jnp.float32)
    numbers = jnp.pad(numbers, (0, 2 * LANES - numbers.shape[0]))
    numbers = jnp.concatenate([numbers, own_traces.reshape(-1)])
    numbers = jnp.pad(numbers, (0, 8 * LANES - numbers.shape[0])).reshape(8, LANES)
    info = gather(numbers, tiles).reshape(tiles, -1)
    base, live_count = info[:, :slots].astype(jnp.int32), info[:, slots : slots + 1].astype(jnp.int32)
    all_traces = info[:, 2 * LANES : 2 * LANES + slots * fh].reshape(tiles, slots, fh)
    z, r, x = base // (rb * xb), (base // xb) % rb, base % xb
    live = jnp.arange(slots, dtype=jnp.int32) < live_count
    plane_ids = jnp.arange(Z, dtype=jnp.int32)
    cover = live[:, None, :] & (z[:, None, :] <= plane_ids[:, None]) & (plane_ids[:, None] < z[:, None, :] + SPAN)
    before = jnp.triu(jnp.ones((slots, slots), jnp.bfloat16), 1)
    rank = jnp.einsum(
        "tzk,kj->tzj", cover.astype(jnp.bfloat16), before, preferred_element_type=jnp.float32
    ).astype(jnp.int32)
    totals = cover.sum(axis=2, dtype=jnp.int32)
    rounds = (jnp.max(totals) + cap - 1) // cap

    first_plane = (me // groups) * planes
    my_place = lax.dynamic_slice_in_dim(jnp.where(cover, rank, -1), first_plane, planes, 1)
    my_totals = lax.dynamic_slice_in_dim(totals, first_plane, planes, 1)
    row_start = jnp.arange(tiles, dtype=jnp.int32)[:, None] * band + PR * r
    col_start = PC * x
    own_z = blocks[:, 0] // (rb * xb)
    own_live = jnp.arange(slots, dtype=jnp.int32) < counts[0]
    own_plane = own_z[:, None] + jnp.arange(SPAN, dtype=jnp.int32)
    own_place = lax.dynamic_index_in_dim(rank, me, 0, False)
    own_place = jnp.where(own_plane[:, :, None] == plane_ids, own_place.T[:, None, :], 0).sum(axis=2)
    source = (own_plane // planes) * groups

    def one_round(number):
        offset = number * cap
        slot_ids = jnp.arange(cap, dtype=jnp.int32) + offset
        hit = my_place[:, :, None] == slot_ids[:, None]
        rows = jnp.where(hit, row_start[:, None, None, :], 0).sum(axis=3)
        cols = jnp.where(hit, col_start[:, None, None, :], 0).sum(axis=3)
        limits = jnp.clip(my_totals - offset, 0, cap)
        received = []
        for d in range(planes):
            sent = extract(
                movie[0], shifts[0], rows[:, d], cols[:, d], limits[:, d], me % groups, cap, step, tiles, d, frames
            )
            received.append(lax.all_to_all(sent, "tile", split_axis=0, concat_axis=0, tiled=True))
        local = own_place - offset
        valid = own_live[:, None] & (local >= 0) & (local < cap)
        index = source * cap + jnp.clip(local, 0, cap - 1)
        return received, index, valid

    def later_round(state):
        number, picked = state
        received, index, valid = one_round(number)
        for d in range(planes):
            fresh = 0
            for g in range(groups):
                fresh = fresh + jnp.take(received[d], index + g * cap, axis=0)
            picked = jnp.where((valid & (own_plane % planes == d))[:, :, None, None], fresh, picked)
        return number + 1, picked

    masked = jnp.where(own_live[:, None, None], footprints, jnp.zeros_like(footprints))
    halves = masked.reshape(slots, SPAN, 2, 2, VOX)
    by_block = lambda part: jnp.transpose(part, (1, 2, 0, 3)).reshape(-1, VOX)
    top = by_block(halves[:, :, 0])
    bottom = by_block(halves[:, :, 1])
    above = lax.ppermute(bottom, "tile", ups)
    below = lax.ppermute(top, "tile", downs)
    trace_above = lax.dynamic_index_in_dim(all_traces, jnp.maximum(me - 1, 0), 0, False)
    trace_below = lax.dynamic_index_in_dim(all_traces, jnp.minimum(me + 1, tiles - 1), 0, False)
    cols = jnp.concatenate([jnp.transpose(masked, (1, 0, 2)).reshape(-1, VOX), above, below], axis=0)

    def edge_ids(neighbour, d, row, shift):
        base_there = lax.dynamic_index_in_dim(base, jnp.clip(neighbour, 0, tiles - 1), 0, False)
        row_there = (base_there // xb) % rb + d
        steps = (jnp.arange(SPAN)[:, None] * rb * xb + d * xb + jnp.arange(2)).reshape(-1, 1).astype(jnp.int32)
        good = (row_there == row) & (neighbour >= 0) & (neighbour < tiles)
        return jnp.where(good, base_there + steps + shift, -1).reshape(-1)

    col_ids = jnp.concatenate(
        [blocks.T.reshape(-1), edge_ids(me - 1, 1, pb, -pb * xb), edge_ids(me + 1, 0, 0, pb * xb)]
    )[None]
    own_ids = blocks.T[:, :, None]
    own_flat = masked.reshape(slots, NB * VOX)

    def columns(own, up, down):
        return jnp.concatenate([jnp.tile(own, (NB, 1)), jnp.tile(up, (NB // 2, 1)), jnp.tile(down, (NB // 2, 1))])

    wide = lambda part: jnp.repeat(part, LANES // fh, axis=1)
    denom_c = overlaps(
        own_flat, own_ids, cols, col_ids, columns(wide(own_traces), wide(trace_above), wide(trace_below))
    )

    pair_feet = masked.reshape(slots * SPAN * 2, 2 * VOX)
    feet = window_feet(pair_feet)
    received, index, valid = one_round(0)
    index = jnp.where(valid, index + (own_plane % planes) * (tiles * cap), -1).reshape(-1)
    _, later = lax.while_loop(
        lambda state: state[0] < rounds,
        later_round,
        (jnp.int32(1), jnp.zeros((slots, SPAN, WIN_R, LANES), jnp.bfloat16)),
    )
    new_wide, numer = update(
        index, feet, later.reshape(-1, WIN_R, LANES), wide(own_traces), denom_c, received, cap, groups
    )
    new = new_wide[:, :: LANES // fh]

    numer = numer.reshape(-1, VOX)
    new_footprints = finish(own_flat, own_ids, cols, col_ids, new_wide, numer, tiles)
    return (new[None], new_footprints.reshape(slots, NB, VOX))


def solution(mesh):
    placed = (
        P("nrn", "tile", None, None),
        P("nrn", "tile", None),
        P("tile", None, None),
        P("tile", None),
        P("nrn", "tile", None),
        P("tile"),
    )
    return jax.shard_map(
        shards,
        mesh=mesh,
        in_specs=placed,
        out_specs=(P("nrn", "tile", None), P("tile", None, None)),
        check_vma=False,
    )
```

```python
import functools

import jax
import jax.numpy as jnp
from jax import lax
from jax.experimental import pallas as pl
from jax.experimental.pallas import tpu as pltpu
from jax.sharding import PartitionSpec as P

Z = 32
PR = 8
PC = 16
VOX = 128
NB = 16
SPAN = 4
LANES = 128
WIN_R = 2 * PR
WIN_C = 2 * PC
EPSILON = 1e-06
MIB = 1 << 20
EXACT = lax.Precision.HIGHEST


def extract_kernel(
    cap, step, tiles, plane, frames, height, width,
    starts_ref, counts_ref, shift_ref, group_ref, movie_ref, out_ref, scr,
):
    frame = pl.program_id(0)

    scr[frame, pl.ds(0, 8), :] = jnp.zeros((8, width + 256), jnp.float32)
    scr[frame, pl.ds(height + 8, 16), :] = jnp.zeros((16, width + 256), jnp.float32)

    @pl.loop(0, height // 32)
    def _(i):
        at = pl.ds(pl.multiple_of(i * 32 + 8, 8), 32)
        scr[frame, at, pl.ds(0, 128)] = jnp.zeros((32, 128), jnp.float32)
        scr[frame, at, pl.ds(width + 128, 128)] = jnp.zeros((32, 128), jnp.float32)
        part = movie_ref[0, pl.ds(pl.multiple_of(i * 32, 32), 32), :]
        scr[frame, at, pl.ds(128, width)] = part.astype(jnp.float32)

    @pl.when(frame == frames - 1)
    def _():
        out_ref[...] = jnp.zeros_like(out_ref)
        lane = lax.broadcasted_iota(jnp.int32, (WIN_R + 8, LANES), 1)
        row = lax.broadcasted_iota(jnp.int32, (WIN_R, LANES), 0)
        first = group_ref[0] * frames
        moves = [
            (shift_ref[2 * (plane * frames + f)], shift_ref[2 * (plane * frames + f) + 1]) for f in range(frames)
        ]

        def one(t, slot):
            start = starts_ref[t, plane * cap + slot]
            r0 = start // width
            c0 = start % width
            window = jnp.zeros((WIN_R, LANES), jnp.float32)
            for f in range(frames):
                down, right = moves[f]
                top = r0 - down + 8
                left = c0 - right + 128
                m = lax.shift_right_logical(left, 7)
                o = left - m * 128
                k = top & 7
                at = pl.ds(pl.multiple_of(top - k, 8), WIN_R + 8)
                near = scr[f, at, pl.ds(pl.multiple_of(m * 128, 128), 128)]
                far = scr[f, at, pl.ds(pl.multiple_of(m * 128 + 128, 128), 128)]
                place = (first + f) * WIN_C
                both = jnp.where(lane >= o, near, far)
                parts = []
                for i in range(0, WIN_R, 8):
                    part = jnp.where(row[:8] >= k, both[i : i + 8], both[i + 8 : i + 16])
                    part = pltpu.roll(part, (8 - k) & 7, 0)
                    parts.append(pltpu.roll(part, (place - o + 128) & 127, 1))
                both = jnp.concatenate(parts, axis=0)
                window = jnp.where((lane[:WIN_R] >= place) & (lane[:WIN_R] < place + WIN_C), both, window)
            return jnp.where(row + r0 < height, window, 0.0).astype(jnp.bfloat16)

        @pl.loop(0, tiles)
        def _(t):
            def some(i, carry):
                slots = [i * step + j for j in range(step)]
                windows = [one(t, slot) for slot in slots]
                for slot, window in zip(slots, windows):
                    out_ref[t * cap + slot] = window
                return carry

            lax.fori_loop(0, (counts_ref[t, plane] + step - 1) // step, some, 0)


def extract(movie, shifts, starts, counts, group, cap, step, tiles, plane, frames):
    _, height, width = movie.shape
    smem = pl.BlockSpec(memory_space=pltpu.SMEM)
    return pl.pallas_call(
        functools.partial(extract_kernel, cap, step, tiles, plane, frames, height, width),
        grid=(frames,),
        in_specs=[smem] * 4 + [pl.BlockSpec((1, height, width), lambda f: (plane * frames + f, 0, 0))],
        out_specs=pl.BlockSpec((tiles * cap, WIN_R, LANES), lambda f: (0, 0, 0)),
        out_shape=jax.ShapeDtypeStruct((tiles * cap, WIN_R, LANES), jnp.bfloat16),
        scratch_shapes=[pltpu.VMEM((frames, height + 24, width + 256), jnp.float32)],
        compiler_params=pltpu.CompilerParams(vmem_limit_bytes=56 * MIB),
        name="extract_windows",
    )(starts, counts, shifts.reshape(-1), group.reshape(1), movie)


def gather_kernel(tiles, own_ref, all_ref, send_sem, recv_sem, own_sem):
    t, p = lax.axis_index("tile"), lax.axis_index("nrn")
    mesh_id = pl.DeviceIdType.MESH
    barrier = pltpu.get_barrier_semaphore()

    def peer(i):
        return lax.rem(t + i, tiles)

    @pl.loop(1, tiles)
    def _(i):
        pl.semaphore_signal(barrier, inc=1, device_id=(peer(i), p), device_id_type=mesh_id)

    pl.semaphore_wait(barrier, tiles - 1)

    def copy(i, slot):
        return pltpu.make_async_remote_copy(
            src_ref=own_ref, dst_ref=all_ref.at[slot], send_sem=send_sem.at[i], recv_sem=recv_sem.at[i],
            device_id=(peer(i), p), device_id_type=mesh_id,
        )

    @pl.loop(1, tiles)
    def _(i):
        copy(i, t).start()

    own = pltpu.make_async_copy(own_ref, all_ref.at[t], own_sem)
    own.start()
    own.wait()

    @pl.loop(1, tiles)
    def _(i):
        copy(i, t).wait_send()
        copy(i, lax.rem(t + tiles - i, tiles)).wait_recv()


def gather(own, tiles):
    vmem = pl.BlockSpec(memory_space=pltpu.VMEM)
    return pl.pallas_call(
        functools.partial(gather_kernel, tiles),
        in_specs=[vmem],
        out_specs=vmem,
        out_shape=jax.ShapeDtypeStruct((tiles,) + own.shape, own.dtype),
        scratch_shapes=[
            pltpu.SemaphoreType.DMA((tiles,)), pltpu.SemaphoreType.DMA((tiles,)), pltpu.SemaphoreType.DMA,
        ],
        compiler_params=pltpu.CompilerParams(collective_id=0, has_side_effects=True),
        name="gather_numbers",
    )(own)


def overlap_kernel(own_ref, own_ids_ref, cols_ref, col_ids_ref, traces_ref, out_ref, acc):
    b = pl.program_id(0)
    products = lax.dot_general(
        own_ref[...], cols_ref[...], (((1,), (1,)), ((), ())), preferred_element_type=jnp.float32
    )
    kept = jnp.where(own_ids_ref[0] == col_ids_ref[...], products, 0.0)

    @pl.when(b == 0)
    def _():
        acc[...] = kept

    @pl.when(b > 0)
    def _():
        acc[...] += kept

    @pl.when(b == pl.num_programs(0) - 1)
    def _():
        out_ref[...] = (
            jnp.dot(acc[...], traces_ref[...], precision=EXACT, preferred_element_type=jnp.float32) + EPSILON
        )


def whole_spec(shape):
    return pl.BlockSpec(shape, lambda i: (0,) * len(shape))


def overlaps(own, own_ids, cols, col_ids, col_traces):
    slots = own.shape[0]
    width = cols.shape[0]
    return pl.pallas_call(
        overlap_kernel,
        grid=(NB,),
        in_specs=[
            pl.BlockSpec((slots, VOX), lambda b: (0, b)),
            pl.BlockSpec((1, slots, 1), lambda b: (b, 0, 0)),
            whole_spec(cols.shape),
            whole_spec(col_ids.shape),
            whole_spec(col_traces.shape),
        ],
        out_specs=whole_spec((slots, LANES)),
        out_shape=jax.ShapeDtypeStruct((slots, LANES), jnp.float32),
        scratch_shapes=[pltpu.VMEM((slots, width), jnp.float32)],
        compiler_params=pltpu.CompilerParams(vmem_limit_bytes=32 * MIB),
        name="denom_c",
    )(own, own_ids, cols, col_ids, col_traces)


def row_keeper(pairs):
    lane = lax.broadcasted_iota(jnp.int32, (pairs, PR, 2 * VOX), 2)
    row = lax.broadcasted_iota(jnp.int32, (pairs, PR, 2 * VOX), 1)
    return (lane & (VOX - 1)) // PC == row


def fold_matrix():
    out_lane = lax.broadcasted_iota(jnp.int32, (LANES, 2 * VOX), 1)
    in_lane = lax.broadcasted_iota(jnp.int32, (LANES, 2 * VOX), 0)
    return ((in_lane & (WIN_C - 1)) == (out_lane // VOX) * PC + (out_lane & (PC - 1))).astype(jnp.bfloat16)


def feet_kernel(masked_ref, out_ref):
    pairs = masked_ref.shape[0]
    feet = masked_ref[...].astype(jnp.float32)
    feet = jnp.where(row_keeper(pairs), feet[:, None, :], 0.0).reshape(pairs * PR, 2 * VOX).astype(jnp.bfloat16)
    feet = lax.dot_general(feet, fold_matrix(), (((1,), (1,)), ((), ())), preferred_element_type=jnp.float32)
    out_ref[...] = feet.astype(jnp.bfloat16)


def window_feet(masked):
    total = masked.shape[0]
    pairs = total // 4
    return pl.pallas_call(
        feet_kernel,
        grid=(4,),
        in_specs=[pl.BlockSpec((pairs, 2 * VOX), lambda i: (i, 0))],
        out_specs=pl.BlockSpec((pairs * PR, LANES), lambda i: (i, 0)),
        out_shape=jax.ShapeDtypeStruct((total * PR, LANES), jnp.bfloat16),
        compiler_params=pltpu.CompilerParams(vmem_limit_bytes=32 * MIB),
        name="window_feet",
    )(masked)


def update_kernel(
    cap, groups, planes, index_ref, feet_ref, extra_ref, traces_ref, denom_ref, *refs
):
    received, (new_ref, numer_ref, windows) = refs[:planes], refs[planes:]
    slots = traces_ref.shape[0]
    count = slots * SPAN
    pairs = count * 2
    length = received[0].shape[0]
    first = pl.program_id(0) * count
    for w in range(count):
        index = index_ref[first + w]
        window = extra_ref[w].astype(jnp.float32)
        for d in range(planes):
            at = jnp.clip(index - d * length, 0, length - 1 - (groups - 1) * cap)
            got = received[d][at].astype(jnp.float32)
            for g in range(1, groups):
                got += received[d][at + g * cap].astype(jnp.float32)
            window = jnp.where(index >= d * length, got, window)
        windows[pl.ds(w * WIN_R, WIN_R), :] = window

    group_a = lax.broadcasted_iota(jnp.int32, (LANES, LANES), 0) // WIN_C
    group_b = lax.broadcasted_iota(jnp.int32, (LANES, LANES), 1) // WIN_C
    group_sum = (group_a == group_b).astype(jnp.float32)
    fold = fold_matrix()
    seen = windows[...]
    sums = (feet_ref[...].astype(jnp.float32) * seen).reshape(slots, SPAN * WIN_R, LANES).sum(axis=1)
    numer_c = jnp.dot(sums, group_sum, precision=EXACT, preferred_element_type=jnp.float32)
    new = traces_ref[...] * numer_c / denom_ref[...]
    new_ref[...] = new
    scaled = (seen.reshape(slots, SPAN * WIN_R, LANES) * new[:, None, :]).reshape(pairs * PR, LANES)
    high = scaled.astype(jnp.bfloat16)
    low = (scaled - high.astype(jnp.float32)).astype(jnp.bfloat16)
    spread = jnp.dot(high, fold, preferred_element_type=jnp.float32)
    spread += jnp.dot(low, fold, preferred_element_type=jnp.float32)
    numer = jnp.where(row_keeper(pairs), spread.reshape(pairs, PR, 2 * VOX), 0.0).sum(axis=1)
    for e in range(2):
        numer_ref[e] = numer[:, e * VOX : (e + 1) * VOX]


def update(index, feet, extra, traces, denom, received, cap, groups):
    slots = traces.shape[0]
    step = 24
    pairs = step * SPAN * 2
    trace_spec = pl.BlockSpec((step, LANES), lambda i: (i, 0))
    numer_spec = pl.BlockSpec((2, pairs, VOX), lambda i: (0, i, 0))
    return pl.pallas_call(
        functools.partial(update_kernel, cap, groups, len(received)),
        grid=(slots // step,),
        in_specs=[
            pl.BlockSpec(memory_space=pltpu.SMEM),
            pl.BlockSpec((pairs * PR, LANES), lambda i: (i, 0)),
            pl.BlockSpec((step * SPAN, WIN_R, LANES), lambda i: (i, 0, 0)),
            trace_spec,
            trace_spec,
        ]
        + [whole_spec(part.shape) for part in received],
        out_specs=[trace_spec, numer_spec],
        out_shape=[
            jax.ShapeDtypeStruct((slots, LANES), jnp.float32),
            jax.ShapeDtypeStruct((2, slots * SPAN * 2, VOX), jnp.float32),
        ],
        scratch_shapes=[pltpu.VMEM((pairs * PR, LANES), jnp.float32)],
        compiler_params=pltpu.CompilerParams(vmem_limit_bytes=48 * MIB),
        name="update_traces",
    )(index, feet, extra, traces, denom, *received)


def finish_kernel(
    tiles, own_in, own_ids_in, cols_in, col_ids_in, new_ref, numer_ref, out_ref,
    own_ref, own_ids_ref, cols_ref, col_ids_ref, near_ref, other_ref, pair, send_sem, recv_sem, load_sem,
):
    operands = ((own_in, own_ref), (own_ids_in, own_ids_ref), (cols_in, cols_ref), (col_ids_in, col_ids_ref))
    loads = [pltpu.make_async_copy(src, dst, load_sem.at[i]) for i, (src, dst) in enumerate(operands)]
    for load in loads:
        load.start()
    t, p = lax.axis_index("tile"), lax.axis_index("nrn")
    q = 1 - p
    has_above, has_below = t > 0, t < tiles - 1
    mesh_id = pl.DeviceIdType.MESH
    barrier = pltpu.get_barrier_semaphore()
    pl.semaphore_signal(barrier, inc=1, device_id=(t, q), device_id_type=mesh_id)

    @pl.when(has_above)
    def _():
        for peer in (p, q):
            pl.semaphore_signal(barrier, inc=1, device_id=(t - 1, peer), device_id_type=mesh_id)

    @pl.when(has_below)
    def _():
        for peer in (p, q):
            pl.semaphore_signal(barrier, inc=1, device_id=(t + 1, peer), device_id_type=mesh_id)

    pl.semaphore_wait(barrier, 1 + 2 * has_above.astype(jnp.int32) + 2 * has_below.astype(jnp.int32))

    def copy(src, dst, i, to):
        return pltpu.make_async_remote_copy(
            src_ref=src, dst_ref=dst, send_sem=send_sem.at[i], recv_sem=recv_sem.at[i],
            device_id=to, device_id_type=mesh_id,
        )

    partner = copy(new_ref, near_ref.at[0], 0, (t, q))
    large = copy(numer_ref, other_ref, 5, (t, q))
    to_below = [copy(new_ref, near_ref.at[1 + i], 1 + i, (t + 1, peer)) for i, peer in enumerate((p, q))]
    to_above = [copy(new_ref, near_ref.at[3 + i], 3 + i, (t - 1, peer)) for i, peer in enumerate((p, q))]

    @pl.when(has_below)
    def _():
        for one in to_below:
            one.start()

    @pl.when(has_above)
    def _():
        for one in to_above:
            one.start()

    partner.start()
    large.start()

    slots = new_ref.shape[0]

    @pl.when(has_below)
    def _():
        for one in to_above:
            one.wait_recv()

    @pl.when(has_above)
    def _():
        for one in to_below:
            one.wait_recv()

    partner.wait()

    def all_frames(mine, other):
        lane = lax.broadcasted_iota(jnp.int32, mine.shape, 1)
        return jnp.where((lane & 1) == p, mine, other)

    own = all_frames(new_ref[...], near_ref[0])
    up = all_frames(near_ref[1], near_ref[2])
    down = all_frames(near_ref[3], near_ref[4])
    columns = jnp.concatenate([own] * NB + [up] * (NB // 2) + [down] * (NB // 2), axis=0)
    both = lax.dot_general(
        own, columns, (((1,), (1,)), ((), ())), precision=EXACT, preferred_element_type=jnp.float32
    )
    pair[...] = both * (2.0 / WIN_C)
    for load in loads:
        load.wait()
    large.wait()

    @pl.loop(0, NB // 2)
    def _(j):
        highs, lows = [], []
        for e in range(2):
            weight = jnp.where(own_ids_ref[2 * j + e] == col_ids_ref[...], pair[...], 0.0)
            highs.append(weight.astype(jnp.bfloat16))
            lows.append((weight - highs[-1].astype(jnp.float32)).astype(jnp.bfloat16))
        sums = jnp.dot(jnp.concatenate(highs + lows, axis=0), cols_ref[...], preferred_element_type=jnp.float32)
        for e in range(2):
            denom = sums[e * slots : (e + 1) * slots] + sums[(e + 2) * slots : (e + 3) * slots]
            at = pl.ds(e * slots * (NB // 2) + j, slots, stride=NB // 2)
            numer = numer_ref[at, :] + other_ref[at, :]
            lanes = pl.ds(pl.multiple_of((2 * j + e) * VOX, VOX), VOX)
            out_ref[:, lanes] = (own_ref[:, lanes].astype(jnp.float32) * numer / (denom + EPSILON)).astype(
                jnp.bfloat16
            )

    @pl.when(has_below)
    def _():
        for one in to_below:
            one.wait_send()

    @pl.when(has_above)
    def _():
        for one in to_above:
            one.wait_send()


def finish(own, own_ids, cols, col_ids, new, numer, tiles):
    vmem = pl.BlockSpec(memory_space=pltpu.VMEM)
    slots, width = own.shape[0], cols.shape[0]
    return pl.pallas_call(
        functools.partial(finish_kernel, tiles),
        in_specs=[pl.BlockSpec(memory_space=pl.ANY)] * 4 + [vmem] * 2,
        out_specs=vmem,
        out_shape=jax.ShapeDtypeStruct(own.shape, jnp.bfloat16),
        scratch_shapes=[pltpu.VMEM(part.shape, part.dtype) for part in (own, own_ids, cols, col_ids)]
        + [
            pltpu.VMEM((5,) + new.shape, jnp.float32),
            pltpu.VMEM(numer.shape, jnp.float32),
            pltpu.VMEM((slots, width), jnp.float32),
            pltpu.SemaphoreType.DMA((6,)),
            pltpu.SemaphoreType.DMA((6,)),
            pltpu.SemaphoreType.DMA((4,)),
        ],
        compiler_params=pltpu.CompilerParams(
            collective_id=1, has_side_effects=True, vmem_limit_bytes=48 * MIB
        ),
        name="new_footprints",
    )(own, own_ids, cols, col_ids, new, numer)


def shards(movie, shifts, footprints, blocks, traces, counts):
    images, height, width = movie.shape[1:]
    tiles, me = lax.axis_size("tile"), lax.axis_index("tile")
    band = height // tiles
    pb = band // PR
    rb, xb = pb + 1, width // PC
    fh, slots = traces.shape[2], footprints.shape[0]
    frames = min(images, fh)
    planes = images // frames
    groups = fh // frames
    cap, step = 25, 5
    ups = [(i, i + 1) for i in range(tiles - 1)]
    downs = [(i + 1, i) for i in range(tiles - 1)]

    own_traces = traces[0]
    numbers = jnp.concatenate([blocks[:, 0], counts]).astype(jnp.float32)
    numbers = jnp.pad(numbers, (0, 2 * LANES - numbers.shape[0]))
    numbers = jnp.concatenate([numbers, own_traces.reshape(-1)])
    numbers = jnp.pad(numbers, (0, 8 * LANES - numbers.shape[0])).reshape(8, LANES)
    info = gather(numbers, tiles).reshape(tiles, -1)
    base, live_count = info[:, :slots].astype(jnp.int32), info[:, slots : slots + 1].astype(jnp.int32)
    all_traces = info[:, 2 * LANES : 2 * LANES + slots * fh].reshape(tiles, slots, fh)
    z, r, x = base // (rb * xb), (base // xb) % rb, base % xb
    live = jnp.arange(slots, dtype=jnp.int32) < live_count
    plane_ids = jnp.arange(Z, dtype=jnp.int32)
    cover = live[:, None, :] & (z[:, None, :] <= plane_ids[:, None]) & (plane_ids[:, None] < z[:, None, :] + SPAN)
    before = jnp.triu(jnp.ones((slots, slots), jnp.bfloat16), 1)
    rank = jnp.einsum(
        "tzk,kj->tzj", cover.astype(jnp.bfloat16), before, preferred_element_type=jnp.float32
    ).astype(jnp.int32)
    totals = cover.sum(axis=2, dtype=jnp.int32)
    rounds = (jnp.max(totals) + cap - 1) // cap

    first_plane = (me // groups) * planes
    my_place = lax.dynamic_slice_in_dim(jnp.where(cover, rank, -1), first_plane, planes, 1)
    my_totals = lax.dynamic_slice_in_dim(totals, first_plane, planes, 1)
    pixel_start = (jnp.arange(tiles, dtype=jnp.int32)[:, None] * band + PR * r) * width + PC * x
    own_z = blocks[:, 0] // (rb * xb)
    own_live = jnp.arange(slots, dtype=jnp.int32) < counts[0]
    own_plane = own_z[:, None] + jnp.arange(SPAN, dtype=jnp.int32)
    own_place = lax.dynamic_index_in_dim(rank, me, 0, False)
    own_place = jnp.where(own_plane[:, :, None] == plane_ids, own_place.T[:, None, :], 0).sum(axis=2)
    source = (own_plane // planes) * groups

    def one_round(number):
        offset = number * cap
        slot_ids = jnp.arange(cap, dtype=jnp.int32) + offset
        hit = my_place[:, :, None] == slot_ids[:, None]
        starts = jnp.where(hit, pixel_start[:, None, None, :], 0).sum(axis=3).reshape(tiles, planes * cap)
        limits = jnp.clip(my_totals - offset, 0, cap)
        received = []
        for d in range(planes):
            sent = extract(
                movie[0], shifts[0], starts, limits, me % groups, cap, step, tiles, d, frames
            )
            received.append(lax.all_to_all(sent, "tile", split_axis=0, concat_axis=0, tiled=True))
        local = own_place - offset
        valid = own_live[:, None] & (local >= 0) & (local < cap)
        index = source * cap + jnp.clip(local, 0, cap - 1)
        return received, index, valid

    def later_round(state):
        number, picked = state
        received, index, valid = one_round(number)
        for d in range(planes):
            fresh = 0
            for g in range(groups):
                fresh = fresh + jnp.take(received[d], index + g * cap, axis=0)
            picked = jnp.where((valid & (own_plane % planes == d))[:, :, None, None], fresh, picked)
        return number + 1, picked

    masked = jnp.where(own_live[:, None, None], footprints, jnp.zeros_like(footprints))
    halves = masked.reshape(slots, SPAN, 2, 2, VOX)
    by_block = lambda part: jnp.transpose(part, (1, 2, 0, 3)).reshape(-1, VOX)
    top = by_block(halves[:, :, 0])
    bottom = by_block(halves[:, :, 1])
    above = lax.ppermute(bottom, "tile", ups)
    below = lax.ppermute(top, "tile", downs)
    trace_above = lax.dynamic_index_in_dim(all_traces, jnp.maximum(me - 1, 0), 0, False)
    trace_below = lax.dynamic_index_in_dim(all_traces, jnp.minimum(me + 1, tiles - 1), 0, False)
    cols = jnp.concatenate([jnp.transpose(masked, (1, 0, 2)).reshape(-1, VOX), above, below], axis=0)

    def edge_ids(neighbour, d, row, shift):
        base_there = lax.dynamic_index_in_dim(base, jnp.clip(neighbour, 0, tiles - 1), 0, False)
        row_there = (base_there // xb) % rb + d
        steps = (jnp.arange(SPAN)[:, None] * rb * xb + d * xb + jnp.arange(2)).reshape(-1, 1).astype(jnp.int32)
        good = (row_there == row) & (neighbour >= 0) & (neighbour < tiles)
        return jnp.where(good, base_there + steps + shift, -1).reshape(-1)

    col_ids = jnp.concatenate(
        [blocks.T.reshape(-1), edge_ids(me - 1, 1, pb, -pb * xb), edge_ids(me + 1, 0, 0, pb * xb)]
    )[None]
    own_ids = blocks.T[:, :, None]
    own_flat = masked.reshape(slots, NB * VOX)

    def columns(own, up, down):
        return jnp.concatenate([jnp.tile(own, (NB, 1)), jnp.tile(up, (NB // 2, 1)), jnp.tile(down, (NB // 2, 1))])

    wide = lambda part: jnp.repeat(part, LANES // fh, axis=1)
    denom_c = overlaps(
        own_flat, own_ids, cols, col_ids, columns(wide(own_traces), wide(trace_above), wide(trace_below))
    )

    pair_feet = masked.reshape(slots * SPAN * 2, 2 * VOX)
    feet = window_feet(pair_feet)
    received, index, valid = one_round(0)
    index = jnp.where(valid, index + (own_plane % planes) * (tiles * cap), -1).reshape(-1)
    zero, denom_c = lax.optimization_barrier((jnp.zeros((1, 1, 1, 1), jnp.bfloat16), denom_c))
    _, later = lax.while_loop(
        lambda state: state[0] < rounds,
        later_round,
        (jnp.int32(1), jnp.broadcast_to(zero, (slots, SPAN, WIN_R, LANES))),
    )
    new_wide, numer = update(
        index, feet, later.reshape(-1, WIN_R, LANES), wide(own_traces), denom_c, received, cap, groups
    )
    new = new_wide[:, :: LANES // fh]

    numer = numer.reshape(-1, VOX)
    new_footprints = finish(own_flat, own_ids, cols, col_ids, new_wide, numer, tiles)
    return (new[None], new_footprints.reshape(slots, NB, VOX))


def solution(mesh):
    placed = (
        P("nrn", "tile", None, None),
        P("nrn", "tile", None),
        P("tile", None, None),
        P("tile", None),
        P("nrn", "tile", None),
        P("tile"),
    )
    return jax.shard_map(
        shards,
        mesh=mesh,
        in_specs=placed,
        out_specs=(P("nrn", "tile", None), P("tile", None, None)),
        check_vma=False,
    )
```
